512 devices in a mesh: hour: 8 (over y, z_hi), sta: 64 (over x, z_lo, core).
Axes of the slice: x: 4, y: 4, z: 16 (z_hi: 2, z_lo: 8; z = z_hi * 8 + z_lo), core: 2. Of those that a mesh axis runs over, the one named last changes fastest.
Arguments:
- records: bfloat16 [8, 1024, 8, 512], P('hour', 'sta'), may hold values from -6 to 6
- masks: int32 [8, 1024, 8], P('hour', 'sta'), may hold values 0 or 1
- plan: int32 [4], replicated, may hold values from 0 to 63
Outputs:
- stacks: bfloat16 [4, 1024, 16, 201], P(None, 'sta', 'hour')
The draws below stay inside these ranges and needn't reach their ends.
All inputs are finite; a program needn't handle non-finite values. No bound on the sum of `masks` on one device may be relied on, other than what follows from the above.
Results may differ from the reference program's by a relative error of at most 0.0055.
Values may be sent and summed in bfloat16 or wider, within the bound.
No kernel may reach another device: no remote copies, remote signals or barrier semaphores. Data moves between devices by JAX's collectives and lax.ppermute only.
A program may use at most 64 MiB of HBM per device.

```python
import math
import jax
import jax.numpy as jnp
from jax import lax

SB = 16
NSEG = 8
SEGLEN = 512
FREQ = 256
LAGS = 201
STEPS = 4
STATIONS = 1024
HOURS = 8
N_HOUR = 8
N_STA = 64


def place_ends(drawn, stream_key, smallest, high):
    longest = drawn.shape.index(max(drawn.shape))
    spots = []
    for shift in (0, 1):
        where = [jax.random.randint(jax.random.fold_in(stream_key, axis), (), 0, length) for axis, length in enumerate(drawn.shape)]
        where[longest] = (where[longest] + shift) % drawn.shape[longest]
        spots.append(tuple(where))
    return drawn.at[spots[0]].set(smallest).at[spots[1]].set(high)


def block_levels(stream_key, dims, split, smallest, largest):
    def one(axis_at, blocks):
        draws = jax.random.uniform(jax.random.fold_in(jax.random.fold_in(stream_key, 6), axis_at), (blocks,), jnp.float32, smallest / len(split), largest / len(split))
        return jnp.repeat(jnp.exp(draws), dims[axis_at] // blocks).reshape((-1,) + (1,) * (len(dims) - axis_at - 1))

    factor_of = one(*split[0])
    for cut in split[1:]:
        factor_of = factor_of * one(*cut)
    return factor_of


def gaussian(stream_key, dims, spread, most, pieces=(), kind=jnp.bfloat16):
    loudness = block_levels(stream_key, dims, pieces, -0.22, 0.18) if pieces else 1.0
    array = jax.random.normal(stream_key, dims, jnp.float32) * spread * loudness
    return jnp.minimum(jnp.maximum(array, -most), most).astype(kind)


def setup_inputs(seed: int = 0) -> dict:
    splits = jax.random.split(jax.random.key(seed), 4)
    records = gaussian(splits[0], (HOURS, STATIONS, NSEG, SEGLEN), 1.0, 6.0, ((0, 8), (1, 64)))
    masks = place_ends((jax.random.randint(splits[1], (HOURS, STATIONS, NSEG), 0, 4) < 3).astype(jnp.int32), jax.random.fold_in(splits[1], 1), 0, 1)
    plan = place_ends(jax.random.randint(splits[2], (STEPS,), 0, N_STA), jax.random.fold_in(splits[2], 1), 0, N_STA - 1).astype(jnp.int32)
    return dict(records=records, masks=masks, plan=plan)


def band_matrix(length, reach):
    places = jnp.arange(length, dtype=jnp.int32)
    return (jnp.abs(places[:, None] - places[None, :]) <= reach).astype(jnp.float32)

def angle_table(first, second, length):
    product = first[:, None] * second[None, :] % length
    return 2.0 * math.pi * product.astype(jnp.float32) / length

def whiten(traces, valid, seglen, nfreq):
    rows = traces.shape[:-1]
    raw = traces.reshape(-1, seglen)
    signal = raw.astype(jnp.float32)
    band_time = band_matrix(seglen, seglen // 8)
    envelope = jnp.dot(jnp.abs(raw), band_time.astype(jnp.bfloat16), preferred_element_type=jnp.float32) / lax.optimization_barrier(jnp.sum(band_time, axis=0)) + 1e-06
    normed = signal / envelope
    angles = angle_table(jnp.arange(seglen, dtype=jnp.int32), jnp.arange(nfreq, dtype=jnp.int32), seglen)
    spec_re = jnp.dot(normed, jnp.cos(angles), precision=lax.Precision.HIGHEST)
    spec_im = -jnp.dot(normed, jnp.sin(angles), precision=lax.Precision.HIGHEST)
    magnitude = jnp.sqrt(spec_re * spec_re + spec_im * spec_im)
    band_freq = band_matrix(nfreq, nfreq // 4)
    smooth = jnp.dot(magnitude, band_freq, precision=lax.Precision.HIGHEST) / lax.optimization_barrier(jnp.sum(band_freq, axis=0)) + 1e-06
    weight = valid.astype(jnp.float32).reshape(-1, 1) / smooth
    white = jnp.stack([spec_re * weight, spec_im * weight])
    return white.reshape((2,) + rows + (nfreq,)).astype(jnp.bfloat16)

def lag_table(nfreq, seglen, nlags, scale):
    shifts = jnp.arange(nlags, dtype=jnp.int32) - nlags // 2
    angles = angle_table(jnp.arange(nfreq, dtype=jnp.int32), shifts, seglen)
    return jnp.concatenate([jnp.cos(angles), -jnp.sin(angles)], axis=0) * scale

def cross_lags(left, right, table):
    left_f = left.astype(jnp.float32)
    right_f = right.astype(jnp.float32)
    real = jnp.einsum('asf,bsf->abf', left_f[0], right_f[0]) + jnp.einsum('asf,bsf->abf', left_f[1], right_f[1])
    imag = jnp.einsum('asf,bsf->abf', left_f[1], right_f[0]) - jnp.einsum('asf,bsf->abf', left_f[0], right_f[1])
    count_a, count_b = (real.shape[0], real.shape[1])
    flat = jnp.concatenate([real, imag], axis=-1).reshape(count_a * count_b, -1)
    return jnp.dot(flat, table, precision=lax.Precision.HIGHEST).reshape(count_a, count_b, table.shape[1])

def reference(records, masks, plan):

    def per_hour(pair):
        return whiten(pair[0], pair[1], SEGLEN, FREQ)
    white = lax.map(per_hour, (records, masks))
    spectra = jnp.transpose(white, (1, 2, 0, 3, 4)).reshape(2, STATIONS, N_HOUR * NSEG, FREQ)
    table = lag_table(FREQ, SEGLEN, LAGS, 1.0 / math.sqrt(NSEG * FREQ * N_HOUR))
    results = []
    for section in range(STEPS):
        source = lax.dynamic_slice_in_dim(spectra, (plan[section] * SB).astype(jnp.int32), SB, 1)

        def per_block(block_index):
            left = lax.dynamic_slice_in_dim(spectra, (block_index * SB).astype(jnp.int32), SB, 1)
            return cross_lags(left, source, table)
        blocks = lax.map(per_block, jnp.arange(N_STA, dtype=jnp.int32))
        results.append(blocks.reshape(STATIONS, SB, LAGS))
    return jnp.stack(results).astype(jnp.bfloat16)
```

```python
import math

import jax
import jax.numpy as jnp
import numpy as np
from jax import lax
from jax.experimental import pallas as pl
from jax.experimental.pallas import tpu as pltpu
from jax.sharding import Mesh, PartitionSpec as P

SB = 16
NSEG = 8
SEGLEN = 512
FREQ = 256
LAGS = 201
STEPS = 4
HOURS = 8
ROWS = SB * NSEG
WIDE = 2 * FREQ
LANES = 128
PAD = 256
PIECE = 2 * NSEG
TILES = WIDE // LANES
GROUP = 32
LINES = 4
SLOTS = 2 * STEPS

F32 = jnp.float32
BF16 = jnp.bfloat16
VMEM_LIMIT = 16 * 1024 * 1024


def angle_rows(times):
    angles = 2.0 * math.pi * ((np.asarray(times)[:, None] * np.arange(FREQ)[None, :]) % SEGLEN) / SEGLEN
    return np.concatenate([np.cos(angles), -np.sin(angles)], axis=1).astype(np.float32)


def lag_tables():
    shifts = np.arange(LAGS) - LAGS // 2
    angles = 2.0 * math.pi * ((np.arange(FREQ)[:, None] * shifts[None, :]) % SEGLEN) / SEGLEN
    table = np.concatenate([np.cos(angles), -np.sin(angles)], axis=0) / math.sqrt(NSEG * FREQ * HOURS)
    table = np.pad(table, ((0, 0), (0, PAD - LAGS)))
    high = table.astype(BF16)
    return high, (table - high.astype(np.float64)).astype(BF16)


def mm(left, right):
    return jnp.dot(left, right, preferred_element_type=F32)


def split(value):
    high = value.astype(BF16)
    return high, (value - high.astype(F32)).astype(BF16)


def band(length, reach):
    first = lax.broadcasted_iota(jnp.int32, (length, length), 0)
    second = lax.broadcasted_iota(jnp.int32, (length, length), 1)
    matrix = jnp.where(jnp.abs(first - second) <= reach, 1.0, 0.0).astype(BF16)
    place = lax.broadcasted_iota(jnp.int32, (1, length), 1)
    count = jnp.minimum(place + reach, length - 1) - jnp.maximum(place - reach, 0) + 1
    return matrix, count.astype(F32)


def whiten_kernel(records, mask, first_rows, turns, white, raw_buffer, trig, sem):
    fetch = pltpu.make_async_copy(records, raw_buffer, sem)
    fetch.start()
    trig[pl.ds(0, NSEG), :] = first_rows[...]
    size, level = NSEG, 0
    while size < SEGLEN:
        cos, sin = trig[pl.ds(0, size), :FREQ], trig[pl.ds(0, size), FREQ:]
        turn_cos, turn_sin = turns[pl.ds(level, 1), :FREQ], turns[pl.ds(level, 1), FREQ:]
        trig[pl.ds(size, size), :FREQ] = cos * turn_cos - sin * turn_sin
        trig[pl.ds(size, size), FREQ:] = sin * turn_cos + cos * turn_sin
        size, level = 2 * size, level + 1
    table_high, table_low = split(trig[...])
    time_band, time_count = band(SEGLEN, SEGLEN // 8)
    freq_band, freq_count = band(FREQ, FREQ // 4)
    fetch.wait()
    raw = raw_buffer[...]
    envelope = mm(jnp.abs(raw), time_band) / time_count + 1e-06
    high, low = split(raw.astype(F32) / envelope)
    spec = mm(high, table_high) + (mm(low, table_high) + mm(high, table_low))
    spec_re, spec_im = spec[:, :FREQ], spec[:, FREQ:]
    magnitude = jnp.sqrt(spec_re * spec_re + spec_im * spec_im)
    high, low = split(magnitude)
    smooth = (mm(high, freq_band) + mm(low, freq_band)) / freq_count + 1e-06
    station = lax.broadcasted_iota(jnp.int32, (SB, NSEG, SB), 0)
    column = lax.broadcasted_iota(jnp.int32, (SB, NSEG, SB), 2)
    spread = jnp.where(station == column, mask[...].astype(F32)[None], 0.0)
    valid = jnp.sum(spread, axis=2, keepdims=True)
    weight = (valid / smooth.reshape(SB, NSEG, FREQ)).reshape(ROWS, FREQ)
    for tile in range(TILES):
        spec_part = (spec_re, spec_im)[tile // 2]
        lanes = slice((tile % 2) * LANES, (tile % 2 + 1) * LANES)
        part = (spec_part[:, lanes] * weight[:, lanes]).astype(BF16)
        for group in range(ROWS // PIECE):
            white[tile * (ROWS // PIECE) + group] = part[group * PIECE : (group + 1) * PIECE]


def whiten(records, masks):
    vmem = pl.BlockSpec(memory_space=pltpu.VMEM)
    return pl.pallas_call(
        whiten_kernel,
        in_specs=[pl.BlockSpec(memory_space=pltpu.HBM), vmem, vmem, vmem],
        out_specs=vmem,
        out_shape=jax.ShapeDtypeStruct((GROUP, PIECE, LANES), BF16),
        scratch_shapes=[
            pltpu.VMEM((ROWS, SEGLEN), BF16),
            pltpu.VMEM((SEGLEN, WIDE), F32),
            pltpu.SemaphoreType.DMA,
        ],
        compiler_params=pltpu.CompilerParams(vmem_limit_bytes=VMEM_LIMIT),
        name="whiten",
    )(records, masks, jnp.asarray(angle_rows(range(NSEG))), jnp.asarray(angle_rows([8, 16, 32, 64, 128, 256, 0, 0])))


def pick_block_kernel(plan, gathered, picked):
    for k in range(STEPS):
        block = plan[k]
        picked[k] = gathered[(block // 16) * 8 + block % 8]


def pick_block(plan, gathered):
    vmem = pl.BlockSpec(memory_space=pltpu.VMEM)
    return pl.pallas_call(
        pick_block_kernel,
        in_specs=[pl.BlockSpec(memory_space=pltpu.SMEM), vmem],
        out_specs=vmem,
        out_shape=jax.ShapeDtypeStruct((STEPS, PIECE, LANES), BF16),
        compiler_params=pltpu.CompilerParams(vmem_limit_bytes=VMEM_LIMIT),
        name="pick_block",
    )(plan, gathered)


def pick_end_kernel(plan, end, mine, other, spread):
    for k in range(STEPS):
        here = (plan[k] // 8) % 2 == end[0]
        piece = jnp.where(here, mine[k].astype(F32), other[k].astype(F32)).astype(BF16)
        for to in range(GROUP // 2):
            spread[to, k] = piece


def pick_end(plan, end, mine, other):
    vmem = pl.BlockSpec(memory_space=pltpu.VMEM)
    smem = pl.BlockSpec(memory_space=pltpu.SMEM)
    return pl.pallas_call(
        pick_end_kernel,
        in_specs=[smem, smem, vmem, vmem],
        out_specs=vmem,
        out_shape=jax.ShapeDtypeStruct((GROUP // 2, STEPS, PIECE, LANES), BF16),
        compiler_params=pltpu.CompilerParams(vmem_limit_bytes=VMEM_LIMIT),
        name="pick_end",
    )(plan, end, mine, other)


def correlate_pairs(core, white, source, table_high, table_low, lagged, own, wide, cross):
    for tile in range(TILES):
        own[tile] = white[pl.ds(tile * 8, 8)].astype(F32).reshape(ROWS, LANES)
        wide[tile] = source[pl.ds(tile * LINES, LINES)].astype(F32).reshape(LINES * STEPS * PIECE, LANES)

    def pair(line, carry):
        for half in range(2):
            right = []
            for s in range(NSEG):
                rows = pl.ds(line * (STEPS * PIECE) + s, SLOTS, stride=NSEG)
                right.append((wide[half, rows, :], wide[half + 2, rows, :]))
            for a in range(SB):
                real = imag = None
                for s in range(NSEG):
                    row = pl.ds(a * NSEG + s, 1)
                    left_re = jnp.broadcast_to(own[half, row, :], (SLOTS, LANES))
                    left_im = jnp.broadcast_to(own[half + 2, row, :], (SLOTS, LANES))
                    right_re, right_im = right[s]
                    add_re = left_re * right_re + left_im * right_im
                    add_im = left_im * right_re - left_re * right_im
                    real = add_re if s == 0 else real + add_re
                    imag = add_im if s == 0 else imag + add_im
                cross[pl.ds(a * SLOTS, SLOTS), pl.ds(half * LANES, LANES)] = real
                cross[pl.ds(a * SLOTS, SLOTS), pl.ds(FREQ + half * LANES, LANES)] = imag
        high, low = split(cross[...])
        out = mm(high, table_high[...]) + (mm(low, table_high[...]) + mm(high, table_low[...]))
        lagged[line * 2 + core] = out.astype(BF16)
        return carry

    lax.fori_loop(0, LINES, pair, 0)


def correlate_near_kernel(core, white, source, table_high, table_low, lagged, own, wide, cross):
    correlate_pairs(core[0], white, source, table_high, table_low, lagged, own, wide, cross)


def correlate_far_kernel(core, near, white, source, table_high, table_low, lagged, own, wide, cross):
    for line in range(LINES):
        lagged[line * 2 + core[0]] = near[line * 2 + core[0]]
    correlate_pairs(1 - core[0], white, source, table_high, table_low, lagged, own, wide, cross)


def correlate(kernel, name, core, *arrays):
    vmem = pl.BlockSpec(memory_space=pltpu.VMEM)
    arrays = arrays + tuple(jnp.asarray(t) for t in lag_tables())
    return pl.pallas_call(
        kernel,
        in_specs=[pl.BlockSpec(memory_space=pltpu.SMEM)] + [vmem] * len(arrays),
        out_specs=vmem,
        out_shape=jax.ShapeDtypeStruct((HOURS, ROWS, PAD), BF16),
        scratch_shapes=[
            pltpu.VMEM((TILES, ROWS, LANES), F32),
            pltpu.VMEM((TILES, LINES * STEPS * PIECE, LANES), F32),
            pltpu.VMEM((ROWS, WIDE), F32),
        ],
        compiler_params=pltpu.CompilerParams(vmem_limit_bytes=VMEM_LIMIT),
        name=name,
    )(core, *arrays)


def shards(records, masks, plan):
    core = lax.axis_index("c").astype(jnp.int32).reshape(1)
    end = lax.axis_index("u").astype(jnp.int32).reshape(1)
    white = whiten(records.reshape(ROWS, SEGLEN), masks[0].T)
    pieces = lax.all_to_all(white, ("x", "v", "c"), 0, 0, tiled=True)
    mine = pick_block(plan, pieces)
    other = lax.ppermute(mine, "u", [(0, 1), (1, 0)])
    spread = pick_end(plan, end, mine, other)
    near = lax.all_to_all(spread, ("x", "v"), 0, 0, tiled=True)
    far = lax.ppermute(near, "c", [(0, 1), (1, 0)])
    lagged = correlate(correlate_near_kernel, "correlate_near", core, white, near)
    lagged = correlate(correlate_far_kernel, "correlate_far", core, lagged, white, far)
    parts = lax.all_to_all(lagged, ("y", "w"), 0, 0, tiled=True)
    total = jnp.sum(parts.astype(F32), axis=0).astype(BF16)
    total = total[:, :LAGS].reshape(SB, STEPS, 2, LAGS)
    return jnp.transpose(total, (1, 0, 2, 3))


def solution(mesh):
    grid = Mesh(mesh.devices.reshape(4, 2, 4, 2, 4, 2), ("y", "w", "x", "u", "v", "c"))
    hour = ("y", "w")
    sta = ("x", "u", "v", "c")
    return jax.shard_map(
        shards,
        mesh=grid,
        in_specs=(P(hour, sta, None, None), P(hour, sta, None), P()),
        out_specs=P(None, sta, hour, None),
        check_vma=False,
    )
```

```python
import math

import jax
import jax.numpy as jnp
import numpy as np
from jax import lax
from jax.experimental import pallas as pl
from jax.experimental.pallas import tpu as pltpu
from jax.sharding import Mesh, PartitionSpec as P

SB = 16
NSEG = 8
SEGLEN = 512
FREQ = 256
LAGS = 201
STEPS = 4
HOURS = 8
ROWS = SB * NSEG
WIDE = 2 * FREQ
LANES = 128
PIECE = 2 * NSEG
TILES = WIDE // LANES
UNITS = 32
LINES = 4
SPREAD = 16
SLOTS = 2 * STEPS
KEPT = 208

F32 = jnp.float32
BF16 = jnp.bfloat16
VMEM_LIMIT = 16 * 1024 * 1024


def angle_rows(times):
    product = (times * lax.broadcasted_iota(jnp.int32, times.shape, 1)) % SEGLEN
    angles = product.astype(F32) * (2.0 * math.pi / SEGLEN)
    return jnp.cos(angles), -jnp.sin(angles)


def lag_tables():
    shifts = np.arange(LAGS) - LAGS // 2
    angles = 2.0 * math.pi * ((shifts[:, None] * np.arange(FREQ)[None, :]) % SEGLEN) / SEGLEN
    table = np.concatenate([np.cos(angles), -np.sin(angles)], axis=1) / math.sqrt(NSEG * FREQ * HOURS)
    table = np.pad(table, ((0, KEPT - LAGS), (0, 0)))
    high = table.astype(BF16)
    return np.concatenate([high, (table - high.astype(np.float64)).astype(BF16)], axis=0)


def mm(left, right):
    return jnp.dot(left, right, preferred_element_type=F32)


def mm_rows(left, right):
    return lax.dot_general(left, right, (((1,), (1,)), ((), ())), preferred_element_type=F32)


def split(value):
    high = value.astype(BF16)
    return high, (value - high.astype(F32)).astype(BF16)


def band(length, reach):
    first = lax.broadcasted_iota(jnp.int32, (length, length), 0)
    second = lax.broadcasted_iota(jnp.int32, (length, length), 1)
    matrix = jnp.where(jnp.abs(first - second) <= reach, 1.0, 0.0).astype(BF16)
    place = lax.broadcasted_iota(jnp.int32, (1, length), 1)
    count = jnp.minimum(place + reach, length - 1) - jnp.maximum(place - reach, 0) + 1
    return matrix, count.astype(F32)


def whiten_kernel(records, mask, white, raw_buffer, mask_buffer, trig, sems):
    fetches = [
        pltpu.make_async_copy(records, raw_buffer, sems.at[0]),
        pltpu.make_async_copy(mask, mask_buffer, sems.at[1]),
    ]
    for fetch in fetches:
        fetch.start()
    row = lax.broadcasted_iota(jnp.int32, (NSEG, FREQ), 0)
    cos, sin = angle_rows(row)
    turns_cos, turns_sin = angle_rows(lax.shift_left(jnp.full_like(row, NSEG), row))
    trig[pl.ds(0, NSEG), :FREQ] = cos
    trig[pl.ds(0, NSEG), FREQ:] = sin
    size, level = NSEG, 0
    while size < SEGLEN:
        cos, sin = trig[pl.ds(0, size), :FREQ], trig[pl.ds(0, size), FREQ:]
        turn_cos, turn_sin = turns_cos[level : level + 1], turns_sin[level : level + 1]
        trig[pl.ds(size, size), :FREQ] = cos * turn_cos - sin * turn_sin
        trig[pl.ds(size, size), FREQ:] = sin * turn_cos + cos * turn_sin
        size, level = 2 * size, level + 1
    table_high, table_low = split(trig[...])
    time_band, time_count = band(SEGLEN, SEGLEN // 8)
    freq_band, freq_count = band(FREQ, FREQ // 4)
    for fetch in fetches:
        fetch.wait()
    raw = raw_buffer[...]
    envelope = mm(jnp.abs(raw), time_band) / time_count + 1e-06
    high, low = split(raw.astype(F32) / envelope)
    spec = mm(high, table_high) + (mm(low, table_high) + mm(high, table_low))
    spec_re, spec_im = spec[:, :FREQ], spec[:, FREQ:]
    magnitude = jnp.sqrt(spec_re * spec_re + spec_im * spec_im)
    high, low = split(magnitude)
    smooth = (mm(high, freq_band) + mm(low, freq_band)) / freq_count + 1e-06
    station = lax.broadcasted_iota(jnp.int32, (SB, NSEG, SB), 0)
    column = lax.broadcasted_iota(jnp.int32, (SB, NSEG, SB), 2)
    spread = jnp.where(station == column, mask_buffer[...].astype(F32)[None], 0.0)
    valid = jnp.sum(spread, axis=2, keepdims=True)
    weight = (valid / smooth.reshape(SB, NSEG, FREQ)).reshape(ROWS, FREQ)
    for tile in range(TILES):
        spec_part = (spec_re, spec_im)[tile // 2]
        lanes = slice((tile % 2) * LANES, (tile % 2 + 1) * LANES)
        part = (spec_part[:, lanes] * weight[:, lanes]).astype(BF16)
        for group in range(ROWS // PIECE):
            white[tile * (ROWS // PIECE) + group] = part[group * PIECE : (group + 1) * PIECE]


def whiten(records, masks):
    hbm = pl.BlockSpec(memory_space=pltpu.HBM)
    return pl.pallas_call(
        whiten_kernel,
        in_specs=[hbm, hbm],
        out_specs=pl.BlockSpec(memory_space=pltpu.VMEM),
        out_shape=jax.ShapeDtypeStruct((UNITS, PIECE, LANES), BF16),
        scratch_shapes=[
            pltpu.VMEM((ROWS, SEGLEN), BF16),
            pltpu.VMEM((NSEG, SB), jnp.int32),
            pltpu.VMEM((SEGLEN, WIDE), F32),
            pltpu.SemaphoreType.DMA((2,)),
        ],
        compiler_params=pltpu.CompilerParams(vmem_limit_bytes=VMEM_LIMIT),
        name="whiten",
    )(records, masks)


def pick_near_kernel(plan, gathered, picked):
    for k in range(STEPS):
        block = plan[k]
        picked[k] = gathered[(block // 16) * 8 + block % 8]


def pick_far_kernel(plan, gathered, spread):
    for k in range(STEPS):
        piece = gathered[(plan[k] // 8) % 2, k]
        for to in range(SPREAD):
            spread[to, k] = piece


def pick(kernel, plan, gathered, shape, name):
    vmem = pl.BlockSpec(memory_space=pltpu.VMEM)
    return pl.pallas_call(
        kernel,
        in_specs=[pl.BlockSpec(memory_space=pltpu.SMEM), vmem],
        out_specs=vmem,
        out_shape=jax.ShapeDtypeStruct(shape, BF16),
        compiler_params=pltpu.CompilerParams(vmem_limit_bytes=VMEM_LIMIT),
        name=name,
    )(plan, gathered)


def correlate_half(core, white, source, table, lagged, own, wide, cross):
    for tile in range(TILES):
        own[tile] = white[pl.ds(tile * 8, 8)].astype(F32).reshape(ROWS, LANES)
        wide[tile] = source[pl.ds(tile * LINES, LINES)].astype(F32).reshape(LINES * STEPS * PIECE, LANES)

    def pair(first, carry):
        for part in range(2):
            line = first * 2 + part
            for half in range(2):
                right = []
                for s in range(NSEG):
                    rows = pl.ds(line * (STEPS * PIECE) + s, SLOTS, stride=NSEG)
                    right.append((wide[half, rows, :], wide[half + 2, rows, :]))
                for a in range(SB):
                    real = imag = None
                    for s in range(NSEG):
                        row = pl.ds(a * NSEG + s, 1)
                        left_re = jnp.broadcast_to(own[half, row, :], (SLOTS, LANES))
                        left_im = jnp.broadcast_to(own[half + 2, row, :], (SLOTS, LANES))
                        right_re, right_im = right[s]
                        add_re = left_re * right_re + left_im * right_im
                        add_im = left_im * right_re - left_re * right_im
                        real = add_re if s == 0 else real + add_re
                        imag = add_im if s == 0 else imag + add_im
                    rows = pl.ds(part * ROWS + a * SLOTS, SLOTS)
                    cross[rows, pl.ds(half * LANES, LANES)] = real
                    cross[rows, pl.ds(FREQ + half * LANES, LANES)] = imag
        high, low = split(cross[...])
        both = mm_rows(table[...], high)
        out = (both[:KEPT] + (both[KEPT:] + mm_rows(table[pl.ds(0, KEPT), :], low))).astype(BF16)
        for part in range(2):
            lagged[first * 2 + part, core] = out[:, part * ROWS : (part + 1) * ROWS]
        return carry

    lax.fori_loop(0, LINES // 2, pair, 0)


def correlate_near_kernel(place, *refs):
    correlate_half(place[0], *refs)


def correlate_far_kernel(place, near, *refs):
    lagged = refs[3]
    for line in range(LINES):
        lagged[line, place[0]] = near[line, place[0]]
    correlate_half(1 - place[0], *refs)


def correlate(kernel, name, place, *arrays):
    vmem = pl.BlockSpec(memory_space=pltpu.VMEM)
    arrays = arrays + (jnp.asarray(lag_tables()),)
    return pl.pallas_call(
        kernel,
        in_specs=[pl.BlockSpec(memory_space=pltpu.SMEM)] + [vmem] * len(arrays),
        out_specs=vmem,
        out_shape=jax.ShapeDtypeStruct((LINES, 2, KEPT, ROWS), BF16),
        scratch_shapes=[
            pltpu.VMEM((TILES, ROWS, LANES), F32),
            pltpu.VMEM((TILES, LINES * STEPS * PIECE, LANES), F32),
            pltpu.VMEM((2 * ROWS, WIDE), F32),
        ],
        compiler_params=pltpu.CompilerParams(vmem_limit_bytes=VMEM_LIMIT),
        name=name,
    )(place, *arrays)


def fold_kernel(place, parts, keep, send):
    mine, other = place[1], 1 - place[1]
    keep_sum, send_sum = parts[0, mine].astype(F32), parts[0, other].astype(F32)
    for quad in range(1, LINES):
        keep_sum = keep_sum + parts[quad, mine].astype(F32)
        send_sum = send_sum + parts[quad, other].astype(F32)
    keep[...] = keep_sum
    send[...] = send_sum.astype(BF16)


def fold(place, parts):
    vmem = pl.BlockSpec(memory_space=pltpu.VMEM)
    return pl.pallas_call(
        fold_kernel,
        in_specs=[pl.BlockSpec(memory_space=pltpu.SMEM), vmem],
        out_specs=[vmem, vmem],
        out_shape=[jax.ShapeDtypeStruct((KEPT, ROWS), F32), jax.ShapeDtypeStruct((KEPT, ROWS), BF16)],
        compiler_params=pltpu.CompilerParams(vmem_limit_bytes=VMEM_LIMIT),
        name="fold",
    )(place, parts)


def finish_kernel(place, keep, both, out):
    total = (keep[...] + both[1 - place[1]].astype(F32)).astype(BF16)
    row = lax.broadcasted_iota(jnp.int32, (ROWS, ROWS), 0)
    column = lax.broadcasted_iota(jnp.int32, (ROWS, ROWS), 1)
    station, slot = (row // 2) % SB, (row // (2 * SB)) * 2 + row % 2
    order = jnp.where(column == station * SLOTS + slot, 1.0, 0.0).astype(BF16)
    out[...] = mm_rows(order, total)[:, :LAGS].astype(BF16)


def finish(place, keep, both):
    vmem = pl.BlockSpec(memory_space=pltpu.VMEM)
    return pl.pallas_call(
        finish_kernel,
        in_specs=[pl.BlockSpec(memory_space=pltpu.SMEM), vmem, vmem],
        out_specs=vmem,
        out_shape=jax.ShapeDtypeStruct((ROWS, LAGS), BF16),
        compiler_params=pltpu.CompilerParams(vmem_limit_bytes=VMEM_LIMIT),
        name="finish",
    )(place, keep, both)


def shards(records, masks, plan):
    place = jnp.stack([lax.axis_index("c"), lax.axis_index("w")]).astype(jnp.int32)
    white = whiten(records.reshape(ROWS, SEGLEN), masks[0].T)
    pieces = lax.all_to_all(white, ("x", "q", "r", "c"), 0, 0, tiled=True)
    picked = pick(pick_near_kernel, plan, pieces, (STEPS, PIECE, LANES), "pick_near")
    ends = lax.all_gather(picked, "p", axis=0, tiled=False)
    spread = pick(pick_far_kernel, plan, ends, (SPREAD, STEPS, PIECE, LANES), "pick_far")
    near = lax.all_to_all(spread, ("x", "q", "r"), 0, 0, tiled=True)
    far = lax.ppermute(near, "c", [(0, 1), (1, 0)])
    lagged = correlate(correlate_near_kernel, "correlate_near", place, white, near)
    lagged = correlate(correlate_far_kernel, "correlate_far", place, lagged, white, far)
    parts = lax.all_to_all(lagged, "y", 0, 0, tiled=True)
    keep, send = fold(place, parts)
    both = lax.all_gather(send, "w", axis=0, tiled=False)
    return finish(place, keep, both).reshape(STEPS, SB, 2, LAGS)


def solution(mesh):
    grid = Mesh(mesh.devices.reshape(4, 2, 4, 2, 2, 2, 2), ("y", "w", "x", "p", "q", "r", "c"))
    hour = ("y", "w")
    sta = ("x", "p", "q", "r", "c")
    return jax.shard_map(
        shards,
        mesh=grid,
        in_specs=(P(hour, sta, None, None), P(hour, sta, None), P()),
        out_specs=P(None, sta, hour, None),
        check_vma=False,
    )
```

```python
import math

import jax
import jax.numpy as jnp
import numpy as np
from jax import lax
from jax.experimental import pallas as pl
from jax.experimental.pallas import tpu as pltpu
from jax.sharding import Mesh, PartitionSpec as P

SB = 16
NSEG = 8
SEGLEN = 512
FREQ = 256
LAGS = 201
STEPS = 4
HOURS = 8
ROWS = SB * NSEG
WIDE = 2 * FREQ
LANES = 128
PIECE = 2 * NSEG
TILES = WIDE // LANES
UNITS = 32
LINES = 4
SPREAD = 16
SLOTS = 2 * STEPS
KEPT = 208

F32 = jnp.float32
BF16 = jnp.bfloat16
VMEM_LIMIT = 16 * 1024 * 1024
WHITEN_LIMIT = 60 * 1024 * 1024


def angle_rows(times):
    product = (times * lax.broadcasted_iota(jnp.int32, times.shape, 1)) % SEGLEN
    angles = product.astype(F32) * (2.0 * math.pi / SEGLEN)
    return jnp.cos(angles), -jnp.sin(angles)


def lag_tables():
    shifts = np.arange(LAGS) - LAGS // 2
    angles = 2.0 * math.pi * ((shifts[:, None] * np.arange(FREQ)[None, :]) % SEGLEN) / SEGLEN
    table = np.concatenate([np.cos(angles), -np.sin(angles)], axis=1) / math.sqrt(NSEG * FREQ * HOURS)
    table = np.pad(table, ((0, KEPT - LAGS), (0, 0)))
    high = table.astype(BF16)
    return np.concatenate([high, (table - high.astype(np.float64)).astype(BF16)], axis=0)


def mm(left, right):
    return jnp.dot(left, right, preferred_element_type=F32)


def mm_rows(left, right):
    return lax.dot_general(left, right, (((1,), (1,)), ((), ())), preferred_element_type=F32)


def split(value):
    high = value.astype(BF16)
    return high, (value - high.astype(F32)).astype(BF16)


def band(length, reach):
    first = lax.broadcasted_iota(jnp.int32, (length, length), 0)
    second = lax.broadcasted_iota(jnp.int32, (length, length), 1)
    matrix = jnp.where(jnp.abs(first - second) <= reach, 1.0, 0.0).astype(BF16)
    place = lax.broadcasted_iota(jnp.int32, (1, length), 1)
    count = jnp.minimum(place + reach, length - 1) - jnp.maximum(place - reach, 0) + 1
    return matrix, count.astype(F32)


def whiten_kernel(records, mask, white, raw_buffer, mask_buffer, trig, sems):
    fetches = [
        pltpu.make_async_copy(records, raw_buffer, sems.at[0]),
        pltpu.make_async_copy(mask, mask_buffer, sems.at[1]),
    ]
    for fetch in fetches:
        fetch.start()
    row = lax.broadcasted_iota(jnp.int32, (NSEG, FREQ), 0)
    cos, sin = angle_rows(row)
    turns_cos, turns_sin = angle_rows(lax.shift_left(jnp.full_like(row, NSEG), row))
    trig[pl.ds(0, NSEG), :FREQ] = cos
    trig[pl.ds(0, NSEG), FREQ:] = sin
    size, level = NSEG, 0
    while size < SEGLEN:
        cos, sin = trig[pl.ds(0, size), :FREQ], trig[pl.ds(0, size), FREQ:]
        turn_cos, turn_sin = turns_cos[level : level + 1], turns_sin[level : level + 1]
        trig[pl.ds(size, size), :FREQ] = cos * turn_cos - sin * turn_sin
        trig[pl.ds(size, size), FREQ:] = sin * turn_cos + cos * turn_sin
        size, level = 2 * size, level + 1
    table_high, table_low = split(trig[...])
    time_band, time_count = band(SEGLEN, SEGLEN // 8)
    freq_band, freq_count = band(FREQ, FREQ // 4)
    for fetch in fetches:
        fetch.wait()
    raw = raw_buffer[...]
    envelope = mm(jnp.abs(raw), time_band) / time_count + 1e-06
    high, low = split(raw.astype(F32) / envelope)
    spec = mm(high, table_high) + (mm(low, table_high) + mm(high, table_low))
    spec_re, spec_im = spec[:, :FREQ], spec[:, FREQ:]
    magnitude = jnp.sqrt(spec_re * spec_re + spec_im * spec_im)
    high, low = split(magnitude)
    smooth = (mm(high, freq_band) + mm(low, freq_band)) / freq_count + 1e-06
    station = lax.broadcasted_iota(jnp.int32, (SB, NSEG, SB), 0)
    column = lax.broadcasted_iota(jnp.int32, (SB, NSEG, SB), 2)
    spread = jnp.where(station == column, mask_buffer[...].astype(F32)[None], 0.0)
    valid = jnp.sum(spread, axis=2, keepdims=True)
    weight = (valid / smooth.reshape(SB, NSEG, FREQ)).reshape(ROWS, FREQ)
    for tile in range(TILES):
        spec_part = (spec_re, spec_im)[tile // 2]
        lanes = slice((tile % 2) * LANES, (tile % 2 + 1) * LANES)
        part = (spec_part[:, lanes] * weight[:, lanes]).astype(BF16)
        for group in range(ROWS // PIECE):
            white[tile * (ROWS // PIECE) + group] = part[group * PIECE : (group + 1) * PIECE]


def whiten(records, masks):
    hbm = pl.BlockSpec(memory_space=pltpu.HBM)
    return pl.pallas_call(
        whiten_kernel,
        in_specs=[hbm, hbm],
        out_specs=pl.BlockSpec(memory_space=pltpu.VMEM),
        out_shape=jax.ShapeDtypeStruct((UNITS, PIECE, LANES), BF16),
        scratch_shapes=[
            pltpu.VMEM((ROWS, SEGLEN), BF16),
            pltpu.VMEM((NSEG, SB), jnp.int32),
            pltpu.VMEM((SEGLEN, WIDE), F32),
            pltpu.SemaphoreType.DMA((2,)),
        ],
        compiler_params=pltpu.CompilerParams(vmem_limit_bytes=WHITEN_LIMIT),
        name="whiten",
    )(records, masks)


def pick_near_kernel(plan, gathered, picked):
    for k in range(STEPS):
        block = plan[k]
        picked[k] = gathered[(block // 16) * 8 + block % 8]


def pick_far_kernel(plan, gathered, spread):
    for k in range(STEPS):
        piece = gathered[(plan[k] // 8) % 2, k]
        for to in range(SPREAD):
            spread[to, k] = piece


def pick(kernel, plan, gathered, shape, name):
    vmem = pl.BlockSpec(memory_space=pltpu.VMEM)
    return pl.pallas_call(
        kernel,
        in_specs=[pl.BlockSpec(memory_space=pltpu.SMEM), vmem],
        out_specs=vmem,
        out_shape=jax.ShapeDtypeStruct(shape, BF16),
        compiler_params=pltpu.CompilerParams(vmem_limit_bytes=VMEM_LIMIT),
        name=name,
    )(plan, gathered)


def correlate_kernel(white, source, table, lagged, own, wide, cross):
    for tile in range(TILES):
        own[tile] = white[pl.ds(tile * 8, 8)].astype(F32).reshape(ROWS, LANES)
        for core in range(2):
            piece = source[core, pl.ds(tile * LINES, LINES)].astype(F32)
            wide[tile, core] = piece.reshape(LINES * STEPS * PIECE, LANES)
    for half in range(2):
        own[TILES + half] = own[half] + own[half + 2]
        wide[TILES + half] = wide[half] - wide[half + 2]

    for line in range(LINES):
        for core in range(2):
            for half in range(2):
                right = []
                for s in range(NSEG):
                    rows = pl.ds(line * (STEPS * PIECE) + s, SLOTS, stride=NSEG)
                    right.append([wide[tile, core, rows, :] for tile in (half, half + 2, half + 4)])
                for a in range(SB):
                    sums = None
                    for s in range(NSEG):
                        row = pl.ds(a * NSEG + s, 1)
                        left = [own[tile, row, :] for tile in (half, half + 2, half + 4)]
                        terms = [jnp.broadcast_to(x, (SLOTS, LANES)) * y for x, y in zip(left, right[s])]
                        sums = terms if sums is None else [x + y for x, y in zip(sums, terms)]
                    re_re, im_im, mixed = sums
                    rows = pl.ds(core * ROWS + a * SLOTS, SLOTS)
                    cross[line, rows, pl.ds(half * LANES, LANES)] = re_re + im_im
                    cross[line, rows, pl.ds(FREQ + half * LANES, LANES)] = mixed + (im_im - re_re)
        high, low = split(cross[line])
        both = mm_rows(table[...], high)
        out = (both[:KEPT] + (both[KEPT:] + mm_rows(table[pl.ds(0, KEPT), :], low))).astype(BF16)
        for core in range(2):
            lagged[line, core] = out[:, core * ROWS : (core + 1) * ROWS]


def correlate(*arrays):
    vmem = pl.BlockSpec(memory_space=pltpu.VMEM)
    arrays = arrays + (jnp.asarray(lag_tables()),)
    return pl.pallas_call(
        correlate_kernel,
        in_specs=[vmem] * len(arrays),
        out_specs=vmem,
        out_shape=jax.ShapeDtypeStruct((LINES, 2, KEPT, ROWS), BF16),
        scratch_shapes=[
            pltpu.VMEM((TILES + 2, ROWS, LANES), F32),
            pltpu.VMEM((TILES + 2, 2, LINES * STEPS * PIECE, LANES), F32),
            pltpu.VMEM((LINES, 2 * ROWS, WIDE), F32),
        ],
        compiler_params=pltpu.CompilerParams(vmem_limit_bytes=VMEM_LIMIT),
        name="correlate",
    )(*arrays)


def fold_kernel(place, parts, keep, send):
    mine, other = place[1], 1 - place[1]
    keep_sum, send_sum = parts[0, mine].astype(F32), parts[0, other].astype(F32)
    for quad in range(1, LINES):
        keep_sum = keep_sum + parts[quad, mine].astype(F32)
        send_sum = send_sum + parts[quad, other].astype(F32)
    keep[...] = keep_sum
    send[...] = send_sum.astype(BF16)


def fold(place, parts):
    vmem = pl.BlockSpec(memory_space=pltpu.VMEM)
    return pl.pallas_call(
        fold_kernel,
        in_specs=[pl.BlockSpec(memory_space=pltpu.SMEM), vmem],
        out_specs=[vmem, vmem],
        out_shape=[jax.ShapeDtypeStruct((KEPT, ROWS), F32), jax.ShapeDtypeStruct((KEPT, ROWS), BF16)],
        compiler_params=pltpu.CompilerParams(vmem_limit_bytes=VMEM_LIMIT),
        name="fold",
    )(place, parts)


def finish_kernel(place, keep, both, out):
    total = (keep[...] + both[1 - place[1]].astype(F32)).astype(BF16)
    row = lax.broadcasted_iota(jnp.int32, (ROWS, ROWS), 0)
    column = lax.broadcasted_iota(jnp.int32, (ROWS, ROWS), 1)
    station, slot = (row // 2) % SB, (row // (2 * SB)) * 2 + row % 2
    order = jnp.where(column == station * SLOTS + slot, 1.0, 0.0).astype(BF16)
    out[...] = mm_rows(order, total)[:, :LAGS].astype(BF16).reshape(STEPS, SB, 2, LAGS)


def finish(place, keep, both):
    vmem = pl.BlockSpec(memory_space=pltpu.VMEM)
    return pl.pallas_call(
        finish_kernel,
        in_specs=[pl.BlockSpec(memory_space=pltpu.SMEM), vmem, vmem],
        out_specs=vmem,
        out_shape=jax.ShapeDtypeStruct((STEPS, SB, 2, LAGS), BF16),
        compiler_params=pltpu.CompilerParams(vmem_limit_bytes=VMEM_LIMIT),
        name="finish",
    )(place, keep, both)


def shards(records, masks, plan):
    place = jnp.stack([lax.axis_index("c"), lax.axis_index("w")]).astype(jnp.int32)
    white = whiten(records.reshape(ROWS, SEGLEN), masks[0].T)
    pieces = lax.all_to_all(white, ("x", "q", "r", "c"), 0, 0, tiled=True)
    picked = pick(pick_near_kernel, plan, pieces, (STEPS, PIECE, LANES), "pick_near")
    ends = lax.all_gather(picked, "p", axis=0, tiled=False)
    spread = pick(pick_far_kernel, plan, ends, (SPREAD, STEPS, PIECE, LANES), "pick_far")
    near = lax.all_to_all(spread, ("x", "q", "r"), 0, 0, tiled=True)
    source = lax.all_gather(near, "c", axis=0, tiled=False)
    lagged = correlate(white, source)
    parts = lax.all_to_all(lagged, "y", 0, 0, tiled=True)
    keep, send = fold(place, parts)
    both = lax.all_gather(send, "w", axis=0, tiled=False)
    return finish(place, keep, both)


def solution(mesh):
    grid = Mesh(mesh.devices.reshape(4, 2, 4, 2, 2, 2, 2), ("y", "w", "x", "p", "q", "r", "c"))
    hour = ("y", "w")
    sta = ("x", "p", "q", "r", "c")
    return jax.shard_map(
        shards,
        mesh=grid,
        in_specs=(P(hour, sta, None, None), P(hour, sta, None), P()),
        out_specs=P(None, sta, hour, None),
        check_vma=False,
    )
```

```python
import math

import jax
import jax.numpy as jnp
import numpy as np
from jax import lax
from jax.experimental import pallas as pl
from jax.experimental.pallas import tpu as pltpu
from jax.sharding import Mesh, PartitionSpec as P

SB = 16
NSEG = 8
SEGLEN = 512
FREQ = 256
LAGS = 201
STEPS = 4
HOURS = 8
ROWS = SB * NSEG
WIDE = 2 * FREQ
LANES = 128
PIECE = 2 * NSEG
TILES = WIDE // LANES
UNITS = 32
LINES = 4
SPREAD = 16
SLOTS = 2 * STEPS
KEPT = 208

F32 = jnp.float32
BF16 = jnp.bfloat16
VMEM_LIMIT = 16 * 1024 * 1024


def angle_rows(times):
    product = (times * lax.broadcasted_iota(jnp.int32, times.shape, 1)) % SEGLEN
    angles = product.astype(F32) * (2.0 * math.pi / SEGLEN)
    return jnp.cos(angles), -jnp.sin(angles)


def lag_tables():
    shifts = np.arange(LAGS) - LAGS // 2
    angles = 2.0 * math.pi * ((shifts[:, None] * np.arange(FREQ)[None, :]) % SEGLEN) / SEGLEN
    table = np.concatenate([np.cos(angles), -np.sin(angles)], axis=1) / math.sqrt(NSEG * FREQ * HOURS)
    table = np.pad(table, ((0, KEPT - LAGS), (0, 0)))
    high = table.astype(BF16)
    return np.concatenate([high, (table - high.astype(np.float64)).astype(BF16)], axis=0)


def mm(left, right):
    return jnp.dot(left, right, preferred_element_type=F32)


def mm_rows(left, right):
    return lax.dot_general(left, right, (((1,), (1,)), ((), ())), preferred_element_type=F32)


def split(value):
    high = value.astype(BF16)
    return high, (value - high.astype(F32)).astype(BF16)


def band(length, reach):
    first = lax.broadcasted_iota(jnp.int32, (length, length), 0)
    second = lax.broadcasted_iota(jnp.int32, (length, length), 1)
    matrix = jnp.where(jnp.abs(first - second) <= reach, 1.0, 0.0).astype(BF16)
    place = lax.broadcasted_iota(jnp.int32, (1, length), 1)
    count = jnp.minimum(place + reach, length - 1) - jnp.maximum(place - reach, 0) + 1
    return matrix, count.astype(F32)


def unit_of(tile, pair):
    return (pair // LINES) * (TILES * LINES) + tile * LINES + pair % LINES


def whiten_kernel(records, mask, plan, white, steps, raw_buffer, mask_buffer, plan_buffer, trig, sems):
    fetches = [
        pltpu.make_async_copy(records, raw_buffer, sems.at[0]),
        pltpu.make_async_copy(mask, mask_buffer, sems.at[1]),
        pltpu.make_async_copy(plan, plan_buffer, sems.at[2]),
    ]
    for fetch in fetches:
        fetch.start()
    row = lax.broadcasted_iota(jnp.int32, (NSEG, FREQ), 0)
    cos, sin = angle_rows(row)
    turns_cos, turns_sin = angle_rows(lax.shift_left(jnp.full_like(row, NSEG), row))
    trig[pl.ds(0, NSEG), :FREQ] = cos
    trig[pl.ds(0, NSEG), FREQ:] = sin
    size, level = NSEG, 0
    while size < SEGLEN:
        cos, sin = trig[pl.ds(0, size), :FREQ], trig[pl.ds(0, size), FREQ:]
        turn_cos, turn_sin = turns_cos[level : level + 1], turns_sin[level : level + 1]
        trig[pl.ds(size, size), :FREQ] = cos * turn_cos - sin * turn_sin
        trig[pl.ds(size, size), FREQ:] = sin * turn_cos + cos * turn_sin
        size, level = 2 * size, level + 1
    table_high, table_low = split(trig[...])
    time_band, time_count = band(SEGLEN, SEGLEN // 8)
    freq_band, freq_count = band(FREQ, FREQ // 4)
    for fetch in fetches:
        fetch.wait()
    raw = raw_buffer[...]
    envelope = mm(jnp.abs(raw), time_band) / time_count + 1e-06
    high, low = split(raw.astype(F32) / envelope)
    spec = mm(high, table_high) + (mm(low, table_high) + mm(high, table_low))
    spec_re, spec_im = spec[:, :FREQ], spec[:, FREQ:]
    magnitude = jnp.sqrt(spec_re * spec_re + spec_im * spec_im)
    high, low = split(magnitude)
    smooth = (mm(high, freq_band) + mm(low, freq_band)) / freq_count + 1e-06
    station = lax.broadcasted_iota(jnp.int32, (SB, NSEG, SB), 0)
    column = lax.broadcasted_iota(jnp.int32, (SB, NSEG, SB), 2)
    spread = jnp.where(station == column, mask_buffer[...].astype(F32)[None], 0.0)
    valid = jnp.sum(spread, axis=2, keepdims=True)
    weight = (valid / smooth.reshape(SB, NSEG, FREQ)).reshape(ROWS, FREQ)
    for tile in range(TILES):
        spec_part = (spec_re, spec_im)[tile // 2]
        lanes = slice((tile % 2) * LANES, (tile % 2 + 1) * LANES)
        part = (spec_part[:, lanes] * weight[:, lanes]).astype(BF16)
        for group in range(ROWS // PIECE):
            white[unit_of(tile, group)] = part[group * PIECE : (group + 1) * PIECE]
    for k in range(STEPS):
        steps[k] = jnp.full((PIECE, LANES), plan_buffer[k], jnp.int32)


def whiten(records, masks, plan):
    hbm = pl.BlockSpec(memory_space=pltpu.HBM)
    vmem = pl.BlockSpec(memory_space=pltpu.VMEM)
    return pl.pallas_call(
        whiten_kernel,
        in_specs=[hbm] * 3,
        out_specs=[vmem] * 2,
        out_shape=[pltpu.VMEM((UNITS, PIECE, LANES), BF16), pltpu.VMEM((STEPS, PIECE, LANES), jnp.int32)],
        scratch_shapes=[
            pltpu.VMEM((ROWS, SEGLEN), BF16),
            pltpu.VMEM((NSEG, SB), jnp.int32),
            pltpu.SMEM((STEPS,), jnp.int32),
            pltpu.VMEM((SEGLEN, WIDE), F32),
            pltpu.SemaphoreType.DMA((3,)),
        ],
        compiler_params=pltpu.CompilerParams(vmem_limit_bytes=VMEM_LIMIT),
        name="whiten",
    )(*(pltpu.with_memory_space_constraint(x, pltpu.HBM) for x in (records, masks, plan)))


def pick_near_kernel(steps, gathered, picked):
    places = []
    for k in range(STEPS):
        block = steps[k]
        q, x, rc = (block // 4) % 2, block // 16, block % 4
        places.append(q * 16 + x * 4 + rc)
    pieces = [jnp.zeros((PIECE, LANES), F32)] * STEPS
    for unit in range(UNITS):
        candidate = gathered[unit].astype(F32)
        pieces = [jnp.where(place == unit, candidate, piece) for place, piece in zip(places, pieces)]
    for k in range(STEPS):
        picked[k] = pieces[k].astype(BF16)


def pick_far_kernel(steps, gathered, spread):
    for k in range(STEPS):
        first = (steps[k] // 8) % 2 == 0
        piece = jnp.where(first, gathered[0, k].astype(F32), gathered[1, k].astype(F32)).astype(BF16)
        for to in range(SPREAD):
            spread[to, k] = piece


def pick(kernel, plan, gathered, shape, name):
    vmem = pl.BlockSpec(memory_space=pltpu.VMEM)
    return pl.pallas_call(
        kernel,
        in_specs=[vmem, vmem],
        out_specs=vmem,
        out_shape=jax.ShapeDtypeStruct(shape, BF16),
        compiler_params=pltpu.CompilerParams(vmem_limit_bytes=VMEM_LIMIT),
        name=name,
    )(plan, gathered)


def correlate_kernel(white, source, table, lagged, own, wide, cross):
    for tile in range(TILES):
        for q in range(2):
            units = white[pl.ds(unit_of(tile, q * LINES), LINES)].astype(F32)
            own[tile, pl.ds(q * (LINES * PIECE), LINES * PIECE), :] = units.reshape(LINES * PIECE, LANES)
            for core in range(2):
                piece = source[core, pl.ds(q * 8 + tile * 2, 2)].astype(F32)
                rows = pl.ds(q * (2 * STEPS * PIECE), 2 * STEPS * PIECE)
                wide[tile, core, rows, :] = piece.reshape(2 * STEPS * PIECE, LANES)
    for half in range(2):
        own[TILES + half] = own[half] + own[half + 2]
        wide[TILES + half] = wide[half] - wide[half + 2]

    for line in range(LINES):
        for core in range(2):
            for half in range(2):
                right = []
                for s in range(NSEG):
                    rows = pl.ds(line * (STEPS * PIECE) + s, SLOTS, stride=NSEG)
                    right.append([wide[tile, core, rows, :] for tile in (half, half + 2, half + 4)])
                for a in range(SB):
                    sums = None
                    for s in range(NSEG):
                        row = pl.ds(a * NSEG + s, 1)
                        left = [own[tile, row, :] for tile in (half, half + 2, half + 4)]
                        terms = [jnp.broadcast_to(x, (SLOTS, LANES)) * y for x, y in zip(left, right[s])]
                        sums = terms if sums is None else [x + y for x, y in zip(sums, terms)]
                    re_re, im_im, mixed = sums
                    rows = pl.ds(core * ROWS + a * SLOTS, SLOTS)
                    cross[line, rows, pl.ds(half * LANES, LANES)] = re_re + im_im
                    cross[line, rows, pl.ds(FREQ + half * LANES, LANES)] = mixed + (im_im - re_re)
        high, low = split(cross[line])
        both = mm_rows(table[...], high)
        out = (both[:KEPT] + (both[KEPT:] + mm_rows(table[pl.ds(0, KEPT), :], low))).astype(BF16)
        for core in range(2):
            lagged[line, core] = out[:, core * ROWS : (core + 1) * ROWS]


def correlate(*arrays):
    vmem = pl.BlockSpec(memory_space=pltpu.VMEM)
    arrays = arrays + (jnp.asarray(lag_tables()),)
    return pl.pallas_call(
        correlate_kernel,
        in_specs=[vmem] * len(arrays),
        out_specs=vmem,
        out_shape=pltpu.VMEM((LINES, 2, KEPT, ROWS), BF16),
        scratch_shapes=[
            pltpu.VMEM((TILES + 2, ROWS, LANES), F32),
            pltpu.VMEM((TILES + 2, 2, LINES * STEPS * PIECE, LANES), F32),
            pltpu.VMEM((LINES, 2 * ROWS, WIDE), F32),
        ],
        compiler_params=pltpu.CompilerParams(vmem_limit_bytes=VMEM_LIMIT),
        name="correlate",
    )(*arrays)


def fold_kernel(place, parts, keep, send):
    mine, other = place[1], 1 - place[1]
    keep_sum, send_sum = parts[0, mine].astype(F32), parts[0, other].astype(F32)
    for quad in range(1, LINES):
        keep_sum = keep_sum + parts[quad, mine].astype(F32)
        send_sum = send_sum + parts[quad, other].astype(F32)
    keep[...] = keep_sum
    send[...] = send_sum.astype(BF16)


def fold(place, parts):
    vmem = pl.BlockSpec(memory_space=pltpu.VMEM)
    return pl.pallas_call(
        fold_kernel,
        in_specs=[pl.BlockSpec(memory_space=pltpu.SMEM), vmem],
        out_specs=[vmem, vmem],
        out_shape=[jax.ShapeDtypeStruct((KEPT, ROWS), F32), jax.ShapeDtypeStruct((KEPT, ROWS), BF16)],
        compiler_params=pltpu.CompilerParams(vmem_limit_bytes=VMEM_LIMIT),
        name="fold",
    )(place, parts)


def finish_kernel(place, keep, both, out):
    total = (keep[...] + both[1 - place[1]].astype(F32)).astype(BF16)
    row = lax.broadcasted_iota(jnp.int32, (ROWS, ROWS), 0)
    column = lax.broadcasted_iota(jnp.int32, (ROWS, ROWS), 1)
    station, slot = (row // 2) % SB, (row // (2 * SB)) * 2 + row % 2
    order = jnp.where(column == station * SLOTS + slot, 1.0, 0.0).astype(BF16)
    out[...] = mm_rows(order, total)[:, :LAGS].astype(BF16).reshape(STEPS, SB, 2, LAGS)


def finish(place, keep, both):
    vmem = pl.BlockSpec(memory_space=pltpu.VMEM)
    return pl.pallas_call(
        finish_kernel,
        in_specs=[pl.BlockSpec(memory_space=pltpu.SMEM), vmem, vmem],
        out_specs=vmem,
        out_shape=jax.ShapeDtypeStruct((STEPS, SB, 2, LAGS), BF16),
        compiler_params=pltpu.CompilerParams(vmem_limit_bytes=VMEM_LIMIT),
        name="finish",
    )(place, keep, both)


def shards(records, masks, plan):
    place = jnp.stack([lax.axis_index("c"), lax.axis_index("w")]).astype(jnp.int32)
    white, steps = whiten(records.reshape(ROWS, SEGLEN), masks[0].T, plan)
    pieces = lax.all_to_all(white, ("q", "x", "r", "c"), 0, 0, tiled=True)
    picked = pick(pick_near_kernel, steps, pieces, (STEPS, PIECE, LANES), "pick_near")
    ends = lax.all_gather(picked, "p", axis=0, tiled=False)
    spread = pick(pick_far_kernel, steps, ends, (SPREAD, STEPS, PIECE, LANES), "pick_far")
    near = lax.all_to_all(spread, ("q", "x", "r"), 0, 0, tiled=True)
    source = lax.all_gather(near, "c", axis=0, tiled=False)
    lagged = correlate(white, source)
    parts = lax.all_to_all(lagged, "y", 0, 0, tiled=True)
    keep, send = fold(place, parts)
    both = lax.all_gather(send, "w", axis=0, tiled=False)
    return finish(place, keep, both)


def solution(mesh):
    grid = Mesh(mesh.devices.reshape(4, 2, 4, 2, 2, 2, 2), ("y", "w", "x", "p", "q", "r", "c"))
    hour = ("y", "w")
    sta = ("x", "p", "q", "r", "c")
    return jax.shard_map(
        shards,
        mesh=grid,
        in_specs=(P(hour, sta, None, None), P(hour, sta, None), P()),
        out_specs=P(None, sta, hour, None),
        check_vma=False,
    )
```

```python
import math

import jax
import jax.numpy as jnp
import numpy as np
from jax import lax
from jax.experimental import pallas as pl
from jax.experimental.pallas import tpu as pltpu
from jax.sharding import Mesh, PartitionSpec as P

SB = 16
NSEG = 8
SEGLEN = 512
FREQ = 256
LAGS = 201
STEPS = 4
HOURS = 8
ROWS = SB * NSEG
WIDE = 2 * FREQ
LANES = 128
PIECE = 2 * NSEG
TILES = WIDE // LANES
UNITS = 32
LINES = 4
SPREAD = 16
SLOTS = 2 * STEPS
KEPT = 208

F32 = jnp.float32
BF16 = jnp.bfloat16
VMEM_LIMIT = 16 * 1024 * 1024


def angle_rows(times):
    product = (times * lax.broadcasted_iota(jnp.int32, times.shape, 1)) % SEGLEN
    angles = product.astype(F32) * (2.0 * math.pi / SEGLEN)
    return jnp.cos(angles), -jnp.sin(angles)


def lag_tables():
    shifts = np.arange(LAGS) - LAGS // 2
    angles = 2.0 * math.pi * ((shifts[:, None] * np.arange(FREQ)[None, :]) % SEGLEN) / SEGLEN
    table = np.concatenate([np.cos(angles), -np.sin(angles)], axis=1) / math.sqrt(NSEG * FREQ * HOURS)
    table = np.pad(table, ((0, KEPT - LAGS), (0, 0)))
    high = table.astype(BF16)
    return np.concatenate([high, (table - high.astype(np.float64)).astype(BF16)], axis=0)


def mm(left, right):
    return jnp.dot(left, right, preferred_element_type=F32)


def mm_rows(left, right):
    return lax.dot_general(left, right, (((1,), (1,)), ((), ())), preferred_element_type=F32)


def split(value):
    high = value.astype(BF16)
    return high, (value - high.astype(F32)).astype(BF16)


def band(length, reach):
    first = lax.broadcasted_iota(jnp.int32, (length, length), 0)
    second = lax.broadcasted_iota(jnp.int32, (length, length), 1)
    matrix = jnp.where(jnp.abs(first - second) <= reach, 1.0, 0.0).astype(BF16)
    place = lax.broadcasted_iota(jnp.int32, (1, length), 1)
    count = jnp.minimum(place + reach, length - 1) - jnp.maximum(place - reach, 0) + 1
    return matrix, count.astype(F32)


def unit_of(tile, pair):
    return (pair // LINES) * (TILES * LINES) + tile * LINES + pair % LINES


def whiten_kernel(records, mask, plan, white, steps, raw_buffer, mask_buffer, plan_buffer, trig, sems):
    fetches = [
        pltpu.make_async_copy(records, raw_buffer, sems.at[0]),
        pltpu.make_async_copy(mask, mask_buffer, sems.at[1]),
        pltpu.make_async_copy(plan, plan_buffer, sems.at[2]),
    ]
    for fetch in fetches:
        fetch.start()
    row = lax.broadcasted_iota(jnp.int32, (NSEG, FREQ), 0)
    cos, sin = angle_rows(row)
    turns_cos, turns_sin = angle_rows(lax.shift_left(jnp.full_like(row, NSEG), row))
    trig[pl.ds(0, NSEG), :FREQ] = cos
    trig[pl.ds(0, NSEG), FREQ:] = sin
    size, level = NSEG, 0
    while size < SEGLEN:
        cos, sin = trig[pl.ds(0, size), :FREQ], trig[pl.ds(0, size), FREQ:]
        turn_cos, turn_sin = turns_cos[level : level + 1], turns_sin[level : level + 1]
        trig[pl.ds(size, size), :FREQ] = cos * turn_cos - sin * turn_sin
        trig[pl.ds(size, size), FREQ:] = sin * turn_cos + cos * turn_sin
        size, level = 2 * size, level + 1
    table_high, table_low = split(trig[...])
    time_band, time_count = band(SEGLEN, SEGLEN // 8)
    freq_band, freq_count = band(FREQ, FREQ // 4)
    for fetch in fetches:
        fetch.wait()
    raw = raw_buffer[...]
    envelope = mm(jnp.abs(raw), time_band) / time_count + 1e-06
    high, low = split(raw.astype(F32) / envelope)
    spec = mm(high, table_high) + (mm(low, table_high) + mm(high, table_low))
    spec_re, spec_im = spec[:, :FREQ], spec[:, FREQ:]
    magnitude = jnp.sqrt(spec_re * spec_re + spec_im * spec_im)
    high, low = split(magnitude)
    smooth = (mm(high, freq_band) + mm(low, freq_band)) / freq_count + 1e-06
    station = lax.broadcasted_iota(jnp.int32, (SB, NSEG, SB), 0)
    column = lax.broadcasted_iota(jnp.int32, (SB, NSEG, SB), 2)
    spread = jnp.where(station == column, mask_buffer[...].astype(F32)[None], 0.0)
    valid = jnp.sum(spread, axis=2, keepdims=True)
    weight = (valid / smooth.reshape(SB, NSEG, FREQ)).reshape(ROWS, FREQ)
    for tile in range(TILES):
        spec_part = (spec_re, spec_im)[tile // 2]
        lanes = slice((tile % 2) * LANES, (tile % 2 + 1) * LANES)
        part = (spec_part[:, lanes] * weight[:, lanes]).astype(BF16)
        for group in range(ROWS // PIECE):
            white[unit_of(tile, group)] = part[group * PIECE : (group + 1) * PIECE]
    for k in range(STEPS):
        steps[k] = jnp.full((PIECE, LANES), plan_buffer[k], jnp.int32)


def whiten(records, masks, plan):
    hbm = pl.BlockSpec(memory_space=pltpu.HBM)
    vmem = pl.BlockSpec(memory_space=pltpu.VMEM)
    return pl.pallas_call(
        whiten_kernel,
        in_specs=[hbm] * 3,
        out_specs=[vmem] * 2,
        out_shape=[pltpu.VMEM((UNITS, PIECE, LANES), BF16), pltpu.VMEM((STEPS, PIECE, LANES), jnp.int32)],
        scratch_shapes=[
            pltpu.VMEM((ROWS, SEGLEN), BF16),
            pltpu.VMEM((NSEG, SB), jnp.int32),
            pltpu.SMEM((STEPS,), jnp.int32),
            pltpu.VMEM((SEGLEN, WIDE), F32),
            pltpu.SemaphoreType.DMA((3,)),
        ],
        compiler_params=pltpu.CompilerParams(vmem_limit_bytes=VMEM_LIMIT),
        name="whiten",
    )(*(pltpu.with_memory_space_constraint(x, pltpu.HBM) for x in (records, masks, plan)))


def pick_near_kernel(steps, gathered, picked):
    places = []
    for k in range(STEPS):
        block = steps[k]
        q, x, rc = (block // 4) % 2, block // 16, block % 4
        places.append(q * 16 + x * 4 + rc)
    pieces = [jnp.zeros((PIECE, LANES), F32)] * STEPS
    for unit in range(UNITS):
        candidate = gathered[unit].astype(F32)
        pieces = [jnp.where(place == unit, candidate, piece) for place, piece in zip(places, pieces)]
    for k in range(STEPS):
        picked[k] = pieces[k].astype(BF16)


def pick_far_kernel(steps, gathered, spread):
    for k in range(STEPS):
        first = (steps[k] // 8) % 2 == 0
        piece = jnp.where(first, gathered[0, k].astype(F32), gathered[1, k].astype(F32)).astype(BF16)
        for to in range(SPREAD):
            spread[to, k] = piece


def pick(kernel, plan, gathered, shape, name):
    vmem = pl.BlockSpec(memory_space=pltpu.VMEM)
    return pl.pallas_call(
        kernel,
        in_specs=[vmem, vmem],
        out_specs=vmem,
        out_shape=jax.ShapeDtypeStruct(shape, BF16),
        compiler_params=pltpu.CompilerParams(vmem_limit_bytes=VMEM_LIMIT),
        name=name,
    )(plan, gathered)


def correlate_kernel(white, source, table, lagged, own, wide, cross):
    for tile in range(TILES):
        for q in range(2):
            units = white[pl.ds(unit_of(tile, q * LINES), LINES)].astype(F32)
            own[tile, pl.ds(q * (LINES * PIECE), LINES * PIECE), :] = units.reshape(LINES * PIECE, LANES)
            for core in range(2):
                piece = source[core, pl.ds(q * 8 + tile * 2, 2)].astype(F32)
                rows = pl.ds(q * (2 * STEPS * PIECE), 2 * STEPS * PIECE)
                wide[tile, core, rows, :] = piece.reshape(2 * STEPS * PIECE, LANES)
    for half in range(2):
        own[TILES + half] = own[half] + own[half + 2]
        wide[TILES + half] = wide[half] - wide[half + 2]

    for line in range(LINES):
        for core in range(2):
            for half in range(2):
                right = []
                for s in range(NSEG):
                    rows = pl.ds(line * (STEPS * PIECE) + s, SLOTS, stride=NSEG)
                    right.append([wide[tile, core, rows, :] for tile in (half, half + 2, half + 4)])
                for a in range(SB):
                    sums = None
                    for s in range(NSEG):
                        row = pl.ds(a * NSEG + s, 1)
                        left = [own[tile, row, :] for tile in (half, half + 2, half + 4)]
                        terms = [jnp.broadcast_to(x, (SLOTS, LANES)) * y for x, y in zip(left, right[s])]
                        sums = terms if sums is None else [x + y for x, y in zip(sums, terms)]
                    re_re, im_im, mixed = sums
                    rows = pl.ds(core * ROWS + a * SLOTS, SLOTS)
                    cross[line, rows, pl.ds(half * LANES, LANES)] = re_re + im_im
                    cross[line, rows, pl.ds(FREQ + half * LANES, LANES)] = mixed + (im_im - re_re)
        high, low = split(cross[line])
        both = mm_rows(table[...], high)
        out = (both[:KEPT] + (both[KEPT:] + mm_rows(table[pl.ds(0, KEPT), :], low))).astype(BF16)
        for core in range(2):
            lagged[line, core] = out[:, core * ROWS : (core + 1) * ROWS]


def correlate(*arrays):
    vmem = pl.BlockSpec(memory_space=pltpu.VMEM)
    arrays = arrays + (jnp.asarray(lag_tables()),)
    return pl.pallas_call(
        correlate_kernel,
        in_specs=[vmem] * len(arrays),
        out_specs=vmem,
        out_shape=pltpu.VMEM((LINES, 2, KEPT, ROWS), BF16),
        scratch_shapes=[
            pltpu.VMEM((TILES + 2, ROWS, LANES), F32),
            pltpu.VMEM((TILES + 2, 2, LINES * STEPS * PIECE, LANES), F32),
            pltpu.VMEM((LINES, 2 * ROWS, WIDE), F32),
        ],
        compiler_params=pltpu.CompilerParams(vmem_limit_bytes=VMEM_LIMIT),
        name="correlate",
    )(*arrays)


def fold_kernel(parts, keep, send):
    mine = lax.axis_index("w")
    other = 1 - mine
    keep_sum, send_sum = parts[0, mine].astype(F32), parts[0, other].astype(F32)
    for quad in range(1, LINES):
        keep_sum = keep_sum + parts[quad, mine].astype(F32)
        send_sum = send_sum + parts[quad, other].astype(F32)
    keep[...] = keep_sum
    send[...] = send_sum.astype(BF16)


def fold(parts):
    vmem = pl.BlockSpec(memory_space=pltpu.VMEM)
    return pl.pallas_call(
        fold_kernel,
        in_specs=[vmem],
        out_specs=[vmem, vmem],
        out_shape=[jax.ShapeDtypeStruct((KEPT, ROWS), F32), jax.ShapeDtypeStruct((KEPT, ROWS), BF16)],
        compiler_params=pltpu.CompilerParams(vmem_limit_bytes=VMEM_LIMIT),
        name="fold",
    )(parts)


def finish_kernel(keep, both, out):
    total = (keep[...] + both[1 - lax.axis_index("w")].astype(F32)).astype(BF16)
    row = lax.broadcasted_iota(jnp.int32, (ROWS, ROWS), 0)
    column = lax.broadcasted_iota(jnp.int32, (ROWS, ROWS), 1)
    station, slot = (row // 2) % SB, (row // (2 * SB)) * 2 + row % 2
    order = jnp.where(column == station * SLOTS + slot, 1.0, 0.0).astype(BF16)
    out[...] = mm_rows(order, total)[:, :LAGS].astype(BF16).reshape(STEPS, SB, 2, LAGS)


def finish(keep, both):
    vmem = pl.BlockSpec(memory_space=pltpu.VMEM)
    return pl.pallas_call(
        finish_kernel,
        in_specs=[vmem, vmem],
        out_specs=vmem,
        out_shape=jax.ShapeDtypeStruct((STEPS, SB, 2, LAGS), BF16),
        compiler_params=pltpu.CompilerParams(vmem_limit_bytes=VMEM_LIMIT),
        name="finish",
    )(keep, both)


def shards(records, masks, plan):
    white, steps = whiten(records.reshape(ROWS, SEGLEN), masks[0].T, plan)
    pieces = lax.all_to_all(white, ("q", "x", "r", "c"), 0, 0, tiled=True)
    picked = pick(pick_near_kernel, steps, pieces, (STEPS, PIECE, LANES), "pick_near")
    ends = lax.all_gather(picked, "p", axis=0, tiled=False)
    spread = pick(pick_far_kernel, steps, ends, (SPREAD, STEPS, PIECE, LANES), "pick_far")
    near = lax.all_to_all(spread, ("q", "x", "r"), 0, 0, tiled=True)
    source = lax.all_gather(near, "c", axis=0, tiled=False)
    lagged = correlate(white, source)
    parts = lax.all_to_all(lagged, "y", 0, 0, tiled=True)
    keep, send = fold(parts)
    both = lax.all_gather(send, "w", axis=0, tiled=False)
    return finish(keep, both)


def solution(mesh):
    grid = Mesh(mesh.devices.reshape(4, 2, 4, 2, 2, 2, 2), ("y", "w", "x", "p", "q", "r", "c"))
    hour = ("y", "w")
    sta = ("x", "p", "q", "r", "c")
    return jax.shard_map(
        shards,
        mesh=grid,
        in_specs=(P(hour, sta, None, None), P(hour, sta, None), P()),
        out_specs=P(None, sta, hour, None),
        check_vma=False,
    )
```

```python
import math

import jax
import jax.numpy as jnp
import numpy as np
from jax import lax
from jax.experimental import pallas as pl
from jax.experimental.pallas import tpu as pltpu
from jax.sharding import Mesh, PartitionSpec as P

SB = 16
NSEG = 8
SEGLEN = 512
FREQ = 256
LAGS = 201
STEPS = 4
HOURS = 8
ROWS = SB * NSEG
WIDE = 2 * FREQ
LANES = 128
PIECE = 2 * NSEG
TILES = WIDE // LANES
UNITS = 32
LINES = 4
SPREAD = 16
SLOTS = 2 * STEPS
KEPT = 208
LAST = KEPT - SLOTS
NEAR = LAGS // 2 - SLOTS // 2

F32 = jnp.float32
BF16 = jnp.bfloat16
VMEM_LIMIT = 16 * 1024 * 1024


def angle_rows(times):
    product = (times * lax.broadcasted_iota(jnp.int32, times.shape, 1)) % SEGLEN
    angles = product.astype(F32) * (2.0 * math.pi / SEGLEN)
    return jnp.cos(angles), -jnp.sin(angles)


def lag_tables():
    shifts = np.arange(LAGS) - LAGS // 2
    angles = 2.0 * math.pi * ((shifts[:, None] * np.arange(FREQ)[None, :]) % SEGLEN) / SEGLEN
    table = np.concatenate([np.cos(angles), -np.sin(angles)], axis=1) / math.sqrt(NSEG * FREQ * HOURS)
    table = np.concatenate([table, table[NEAR + 1 : NEAR + SLOTS]], axis=0)
    high = table.astype(BF16)
    return np.concatenate([high, (table - high.astype(np.float64)).astype(BF16)], axis=0)


def mm(left, right):
    return jnp.dot(left, right, preferred_element_type=F32)


def mm_rows(left, right):
    return lax.dot_general(left, right, (((1,), (1,)), ((), ())), preferred_element_type=F32)


def spare():
    return lax.broadcasted_iota(jnp.int32, (SLOTS, ROWS), 0) > 0


def pack(value, near):
    high = value.astype(BF16)
    rest = near - near.astype(BF16).astype(F32)
    last = jnp.where(spare(), rest, value[LAST:])
    return jnp.concatenate([high[: LAST - SLOTS], jnp.concatenate([value[LAST - SLOTS : LAST], last], axis=0).astype(BF16)], axis=0)


def unpack(value):
    near = value[NEAR : NEAR + SLOTS] + jnp.where(spare(), value[LAST:], 0.0)
    return jnp.concatenate([value[:NEAR], near, value[NEAR + SLOTS :]], axis=0)


def split(value):
    high = value.astype(BF16)
    return high, (value - high.astype(F32)).astype(BF16)


def band(length, reach):
    first = lax.broadcasted_iota(jnp.int32, (length, length), 0)
    second = lax.broadcasted_iota(jnp.int32, (length, length), 1)
    matrix = jnp.where(jnp.abs(first - second) <= reach, 1.0, 0.0).astype(BF16)
    place = lax.broadcasted_iota(jnp.int32, (1, length), 1)
    count = jnp.minimum(place + reach, length - 1) - jnp.maximum(place - reach, 0) + 1
    return matrix, count.astype(F32)


def unit_of(tile, pair):
    return (pair // LINES) * (TILES * LINES) + tile * LINES + pair % LINES


def whiten_kernel(records, mask, plan, white, steps, raw_buffer, mask_buffer, plan_buffer, trig, sems):
    fetches = [
        pltpu.make_async_copy(records, raw_buffer, sems.at[0]),
        pltpu.make_async_copy(mask, mask_buffer, sems.at[1]),
        pltpu.make_async_copy(plan, plan_buffer, sems.at[2]),
    ]
    for fetch in fetches:
        fetch.start()
    row = lax.broadcasted_iota(jnp.int32, (NSEG, FREQ), 0)
    cos, sin = angle_rows(row)
    turns_cos, turns_sin = angle_rows(lax.shift_left(jnp.full_like(row, NSEG), row))
    trig[pl.ds(0, NSEG), :FREQ] = cos
    trig[pl.ds(0, NSEG), FREQ:] = sin
    size, level = NSEG, 0
    while size < SEGLEN:
        cos, sin = trig[pl.ds(0, size), :FREQ], trig[pl.ds(0, size), FREQ:]
        turn_cos, turn_sin = turns_cos[level : level + 1], turns_sin[level : level + 1]
        trig[pl.ds(size, size), :FREQ] = cos * turn_cos - sin * turn_sin
        trig[pl.ds(size, size), FREQ:] = sin * turn_cos + cos * turn_sin
        size, level = 2 * size, level + 1
    table_high, table_low = split(trig[...])
    time_band, time_count = band(SEGLEN, SEGLEN // 8)
    freq_band, freq_count = band(FREQ, FREQ // 4)
    for fetch in fetches:
        fetch.wait()
    raw = raw_buffer[...]
    envelope = mm(jnp.abs(raw), time_band) / time_count + 1e-06
    high, low = split(raw.astype(F32) / envelope)
    spec = mm(high, table_high) + (mm(low, table_high) + mm(high, table_low))
    spec_re, spec_im = spec[:, :FREQ], spec[:, FREQ:]
    magnitude = jnp.sqrt(spec_re * spec_re + spec_im * spec_im)
    high, low = split(magnitude)
    smooth = (mm(high, freq_band) + mm(low, freq_band)) / freq_count + 1e-06
    station = lax.broadcasted_iota(jnp.int32, (SB, NSEG, SB), 0)
    column = lax.broadcasted_iota(jnp.int32, (SB, NSEG, SB), 2)
    spread = jnp.where(station == column, mask_buffer[...].astype(F32)[None], 0.0)
    valid = jnp.sum(spread, axis=2, keepdims=True)
    weight = (valid / smooth.reshape(SB, NSEG, FREQ)).reshape(ROWS, FREQ)
    for tile in range(TILES):
        spec_part = (spec_re, spec_im)[tile // 2]
        lanes = slice((tile % 2) * LANES, (tile % 2 + 1) * LANES)
        part = (spec_part[:, lanes] * weight[:, lanes]).astype(BF16)
        for group in range(ROWS // PIECE):
            white[unit_of(tile, group)] = part[group * PIECE : (group + 1) * PIECE]
    for k in range(STEPS):
        steps[k] = jnp.full((PIECE, LANES), plan_buffer[k], jnp.int32)


def whiten(records, masks, plan):
    hbm = pl.BlockSpec(memory_space=pltpu.HBM)
    vmem = pl.BlockSpec(memory_space=pltpu.VMEM)
    return pl.pallas_call(
        whiten_kernel,
        in_specs=[hbm] * 3,
        out_specs=[vmem] * 2,
        out_shape=[pltpu.VMEM((UNITS, PIECE, LANES), BF16), pltpu.VMEM((STEPS, PIECE, LANES), jnp.int32)],
        scratch_shapes=[
            pltpu.VMEM((ROWS, SEGLEN), BF16),
            pltpu.VMEM((NSEG, SB), jnp.int32),
            pltpu.SMEM((STEPS,), jnp.int32),
            pltpu.VMEM((SEGLEN, WIDE), F32),
            pltpu.SemaphoreType.DMA((3,)),
        ],
        compiler_params=pltpu.CompilerParams(vmem_limit_bytes=VMEM_LIMIT),
        name="whiten",
    )(*(pltpu.with_memory_space_constraint(x, pltpu.HBM) for x in (records, masks, plan)))


def pick_near_kernel(steps, gathered, picked):
    places = []
    for k in range(STEPS):
        block = steps[k]
        q, x, rc = (block // 4) % 2, block // 16, block % 4
        places.append(q * 16 + x * 4 + rc)
    pieces = [jnp.zeros((PIECE, LANES), F32)] * STEPS
    for unit in range(UNITS):
        candidate = gathered[unit].astype(F32)
        pieces = [jnp.where(place == unit, candidate, piece) for place, piece in zip(places, pieces)]
    for k in range(STEPS):
        picked[k] = pieces[k].astype(BF16)


def pick_far_kernel(steps, gathered, spread):
    for k in range(STEPS):
        first = (steps[k] // 8) % 2 == 0
        piece = jnp.where(first, gathered[0, k].astype(F32), gathered[1, k].astype(F32)).astype(BF16)
        for to in range(SPREAD):
            spread[to, k] = piece


def pick(kernel, plan, gathered, shape, name):
    vmem = pl.BlockSpec(memory_space=pltpu.VMEM)
    return pl.pallas_call(
        kernel,
        in_specs=[vmem, vmem],
        out_specs=vmem,
        out_shape=jax.ShapeDtypeStruct(shape, BF16),
        compiler_params=pltpu.CompilerParams(vmem_limit_bytes=VMEM_LIMIT),
        name=name,
    )(plan, gathered)


def correlate_kernel(white, source, table, lagged, own, wide, cross):
    for tile in range(TILES):
        for q in range(2):
            units = white[pl.ds(unit_of(tile, q * LINES), LINES)].astype(F32)
            own[tile, pl.ds(q * (LINES * PIECE), LINES * PIECE), :] = units.reshape(LINES * PIECE, LANES)
            for core in range(2):
                piece = source[core, pl.ds(q * 8 + tile * 2, 2)].astype(F32)
                rows = pl.ds(q * (2 * STEPS * PIECE), 2 * STEPS * PIECE)
                wide[tile, core, rows, :] = piece.reshape(2 * STEPS * PIECE, LANES)
    for half in range(2):
        own[TILES + half] = own[half] + own[half + 2]
        wide[TILES + half] = wide[half] - wide[half + 2]

    for line in range(LINES):
        for core in range(2):
            for half in range(2):
                right = []
                for s in range(NSEG):
                    rows = pl.ds(line * (STEPS * PIECE) + s, SLOTS, stride=NSEG)
                    right.append([wide[tile, core, rows, :] for tile in (half, half + 2, half + 4)])
                for a in range(SB):
                    sums = None
                    for s in range(NSEG):
                        row = pl.ds(a * NSEG + s, 1)
                        left = [own[tile, row, :] for tile in (half, half + 2, half + 4)]
                        terms = [jnp.broadcast_to(x, (SLOTS, LANES)) * y for x, y in zip(left, right[s])]
                        sums = terms if sums is None else [x + y for x, y in zip(sums, terms)]
                    re_re, im_im, mixed = sums
                    rows = pl.ds(core * ROWS + a * SLOTS, SLOTS)
                    cross[line, rows, pl.ds(half * LANES, LANES)] = re_re + im_im
                    cross[line, rows, pl.ds(FREQ + half * LANES, LANES)] = mixed + (im_im - re_re)
        high, low = split(cross[line])
        both = mm_rows(table[...], high)
        out = both[:KEPT] + (both[KEPT:] + mm_rows(table[pl.ds(0, KEPT), :], low))
        for core in range(2):
            part = out[:, core * ROWS : (core + 1) * ROWS]
            lagged[line, core] = pack(part, part[LAST:])


def correlate(*arrays):
    vmem = pl.BlockSpec(memory_space=pltpu.VMEM)
    arrays = arrays + (jnp.asarray(lag_tables()),)
    return pl.pallas_call(
        correlate_kernel,
        in_specs=[vmem] * len(arrays),
        out_specs=vmem,
        out_shape=pltpu.VMEM((LINES, 2, KEPT, ROWS), BF16),
        scratch_shapes=[
            pltpu.VMEM((TILES + 2, ROWS, LANES), F32),
            pltpu.VMEM((TILES + 2, 2, LINES * STEPS * PIECE, LANES), F32),
            pltpu.VMEM((LINES, 2 * ROWS, WIDE), F32),
        ],
        compiler_params=pltpu.CompilerParams(vmem_limit_bytes=VMEM_LIMIT),
        name="correlate",
    )(*arrays)


def fold_kernel(parts, keep, send):
    mine = lax.axis_index("w")
    other = 1 - mine
    keep_sum, send_sum = parts[0, mine].astype(F32), parts[0, other].astype(F32)
    for quad in range(1, LINES):
        keep_sum = keep_sum + parts[quad, mine].astype(F32)
        send_sum = send_sum + parts[quad, other].astype(F32)
    keep[...] = unpack(keep_sum)
    send_sum = unpack(send_sum)
    send[...] = pack(send_sum, send_sum[NEAR : NEAR + SLOTS])


def fold(parts):
    vmem = pl.BlockSpec(memory_space=pltpu.VMEM)
    return pl.pallas_call(
        fold_kernel,
        in_specs=[vmem],
        out_specs=[vmem, vmem],
        out_shape=[jax.ShapeDtypeStruct((KEPT, ROWS), F32), jax.ShapeDtypeStruct((KEPT, ROWS), BF16)],
        compiler_params=pltpu.CompilerParams(vmem_limit_bytes=VMEM_LIMIT),
        name="fold",
    )(parts)


def finish_kernel(keep, both, out):
    total = (keep[...] + unpack(both[1 - lax.axis_index("w")].astype(F32))).astype(BF16)
    row = lax.broadcasted_iota(jnp.int32, (ROWS, ROWS), 0)
    column = lax.broadcasted_iota(jnp.int32, (ROWS, ROWS), 1)
    station, slot = (row // 2) % SB, (row // (2 * SB)) * 2 + row % 2
    order = jnp.where(column == station * SLOTS + slot, 1.0, 0.0).astype(BF16)
    out[...] = mm_rows(order, total)[:, :LAGS].astype(BF16).reshape(STEPS, SB, 2, LAGS)


def finish(keep, both):
    vmem = pl.BlockSpec(memory_space=pltpu.VMEM)
    return pl.pallas_call(
        finish_kernel,
        in_specs=[vmem, vmem],
        out_specs=vmem,
        out_shape=jax.ShapeDtypeStruct((STEPS, SB, 2, LAGS), BF16),
        compiler_params=pltpu.CompilerParams(vmem_limit_bytes=VMEM_LIMIT),
        name="finish",
    )(keep, both)


def shards(records, masks, plan):
    white, steps = whiten(records.reshape(ROWS, SEGLEN), masks[0].T, plan)
    pieces = lax.all_to_all(white, ("q", "x", "r", "c"), 0, 0, tiled=True)
    picked = pick(pick_near_kernel, steps, pieces, (STEPS, PIECE, LANES), "pick_near")
    ends = lax.all_gather(picked, "p", axis=0, tiled=False)
    spread = pick(pick_far_kernel, steps, ends, (SPREAD, STEPS, PIECE, LANES), "pick_far")
    near = lax.all_to_all(spread, ("q", "x", "r"), 0, 0, tiled=True)
    source = lax.all_gather(near, "c", axis=0, tiled=False)
    lagged = correlate(white, source)
    parts = lax.all_to_all(lagged, "y", 0, 0, tiled=True)
    keep, send = fold(parts)
    both = lax.all_gather(send, "w", axis=0, tiled=False)
    return finish(keep, both)


def solution(mesh):
    grid = Mesh(mesh.devices.reshape(4, 2, 4, 2, 2, 2, 2), ("y", "w", "x", "p", "q", "r", "c"))
    hour = ("y", "w")
    sta = ("x", "p", "q", "r", "c")
    return jax.shard_map(
        shards,
        mesh=grid,
        in_specs=(P(hour, sta, None, None), P(hour, sta, None), P()),
        out_specs=P(None, sta, hour, None),
        check_vma=False,
    )
```

```python
import math

import jax
import jax.numpy as jnp
import numpy as np
from jax import lax
from jax.experimental import pallas as pl
from jax.experimental.pallas import tpu as pltpu
from jax.sharding import Mesh, PartitionSpec as P

SB = 16
NSEG = 8
SEGLEN = 512
FREQ = 256
LAGS = 201
STEPS = 4
HOURS = 8
ROWS = SB * NSEG
WIDE = 2 * FREQ
LANES = 128
PIECE = 2 * NSEG
TILES = WIDE // LANES
UNITS = 32
LINES = 4
SPREAD = 16
SLOTS = 2 * STEPS
KEPT = 208
LAST = KEPT - SLOTS
NEAR = LAGS // 2 - SLOTS // 2

F32 = jnp.float32
BF16 = jnp.bfloat16
VMEM_LIMIT = 16 * 1024 * 1024


def angle_rows(times):
    product = (times * lax.broadcasted_iota(jnp.int32, times.shape, 1)) % SEGLEN
    angles = product.astype(F32) * (2.0 * math.pi / SEGLEN)
    return jnp.cos(angles), -jnp.sin(angles)


def lag_tables():
    shifts = np.arange(LAGS) - LAGS // 2
    angles = 2.0 * math.pi * ((shifts[:, None] * np.arange(FREQ)[None, :]) % SEGLEN) / SEGLEN
    table = np.concatenate([np.cos(angles), -np.sin(angles)], axis=1) / math.sqrt(NSEG * FREQ * HOURS)
    table = np.concatenate([table, table[NEAR + 1 : NEAR + SLOTS]], axis=0)
    high = table.astype(BF16)
    return np.concatenate([high, (table - high.astype(np.float64)).astype(BF16)], axis=0)


def mm(left, right):
    return jnp.dot(left, right, preferred_element_type=F32)


def mm_rows(left, right):
    return lax.dot_general(left, right, (((1,), (1,)), ((), ())), preferred_element_type=F32)


def spare():
    return lax.broadcasted_iota(jnp.int32, (SLOTS, ROWS), 0) > 0


def pack(value, near):
    high = value.astype(BF16)
    rest = near - near.astype(BF16).astype(F32)
    last = jnp.where(spare(), rest, value[LAST:])
    return jnp.concatenate([high[: LAST - SLOTS], jnp.concatenate([value[LAST - SLOTS : LAST], last], axis=0).astype(BF16)], axis=0)


def unpack(value):
    near = value[NEAR : NEAR + SLOTS] + jnp.where(spare(), value[LAST:], 0.0)
    return jnp.concatenate([value[:NEAR], near, value[NEAR + SLOTS :]], axis=0)


def split(value):
    high = value.astype(BF16)
    return high, (value - high.astype(F32)).astype(BF16)


def band(length, reach):
    first = lax.broadcasted_iota(jnp.int32, (length, length), 0)
    second = lax.broadcasted_iota(jnp.int32, (length, length), 1)
    matrix = jnp.where(jnp.abs(first - second) <= reach, 1.0, 0.0).astype(BF16)
    place = lax.broadcasted_iota(jnp.int32, (1, length), 1)
    count = jnp.minimum(place + reach, length - 1) - jnp.maximum(place - reach, 0) + 1
    return matrix, count.astype(F32)


def unit_of(tile, pair):
    return (pair // LINES) * (TILES * LINES) + tile * LINES + pair % LINES


def whiten_kernel(records, mask, plan, white, steps, raw_buffer, mask_buffer, plan_buffer, trig, sems):
    fetches = [
        pltpu.make_async_copy(records, raw_buffer, sems.at[0]),
        pltpu.make_async_copy(mask, mask_buffer, sems.at[1]),
        pltpu.make_async_copy(plan, plan_buffer, sems.at[2]),
    ]
    for fetch in fetches:
        fetch.start()
    row = lax.broadcasted_iota(jnp.int32, (NSEG, FREQ), 0)
    cos, sin = angle_rows(row)
    turns_cos, turns_sin = angle_rows(lax.shift_left(jnp.full_like(row, NSEG), row))
    trig[pl.ds(0, NSEG), :FREQ] = cos
    trig[pl.ds(0, NSEG), FREQ:] = sin
    size, level = NSEG, 0
    while size < SEGLEN:
        cos, sin = trig[pl.ds(0, size), :FREQ], trig[pl.ds(0, size), FREQ:]
        turn_cos, turn_sin = turns_cos[level : level + 1], turns_sin[level : level + 1]
        trig[pl.ds(size, size), :FREQ] = cos * turn_cos - sin * turn_sin
        trig[pl.ds(size, size), FREQ:] = sin * turn_cos + cos * turn_sin
        size, level = 2 * size, level + 1
    table_high, table_low = split(trig[...])
    time_band, time_count = band(SEGLEN, SEGLEN // 8)
    freq_band, freq_count = band(FREQ, FREQ // 4)
    for fetch in fetches:
        fetch.wait()
    raw = raw_buffer[...]
    envelope = mm(jnp.abs(raw), time_band) / time_count + 1e-06
    high, low = split(raw.astype(F32) / envelope)
    spec = mm(high, table_high) + (mm(low, table_high) + mm(high, table_low))
    spec_re, spec_im = spec[:, :FREQ], spec[:, FREQ:]
    magnitude = jnp.sqrt(spec_re * spec_re + spec_im * spec_im)
    high, low = split(magnitude)
    smooth = (mm(high, freq_band) + mm(low, freq_band)) / freq_count + 1e-06
    station = lax.broadcasted_iota(jnp.int32, (SB, NSEG, SB), 0)
    column = lax.broadcasted_iota(jnp.int32, (SB, NSEG, SB), 2)
    spread = jnp.where(station == column, mask_buffer[...].astype(F32)[None], 0.0)
    valid = jnp.sum(spread, axis=2, keepdims=True)
    weight = (valid / smooth.reshape(SB, NSEG, FREQ)).reshape(ROWS, FREQ)
    for tile in range(TILES):
        spec_part = (spec_re, spec_im)[tile // 2]
        lanes = slice((tile % 2) * LANES, (tile % 2 + 1) * LANES)
        part = (spec_part[:, lanes] * weight[:, lanes]).astype(BF16)
        for group in range(ROWS // PIECE):
            white[unit_of(tile, group)] = part[group * PIECE : (group + 1) * PIECE]
    for k in range(STEPS):
        steps[k] = jnp.full((PIECE, LANES), plan_buffer[k], jnp.int32)


def whiten(records, masks, plan):
    hbm = pl.BlockSpec(memory_space=pltpu.HBM)
    vmem = pl.BlockSpec(memory_space=pltpu.VMEM)
    return pl.pallas_call(
        whiten_kernel,
        in_specs=[hbm] * 3,
        out_specs=[vmem] * 2,
        out_shape=[pltpu.VMEM((UNITS, PIECE, LANES), BF16), pltpu.VMEM((STEPS, PIECE, LANES), jnp.int32)],
        scratch_shapes=[
            pltpu.VMEM((ROWS, SEGLEN), BF16),
            pltpu.VMEM((NSEG, SB), jnp.int32),
            pltpu.SMEM((STEPS,), jnp.int32),
            pltpu.VMEM((SEGLEN, WIDE), F32),
            pltpu.SemaphoreType.DMA((3,)),
        ],
        compiler_params=pltpu.CompilerParams(vmem_limit_bytes=VMEM_LIMIT),
        name="whiten",
    )(*(pltpu.with_memory_space_constraint(x, pltpu.HBM) for x in (records, masks, plan)))


def pick_near_kernel(steps, gathered, picked):
    places = []
    for k in range(STEPS):
        block = steps[k]
        q, x, rc = (block // 4) % 2, block // 16, block % 4
        places.append(q * 16 + x * 4 + rc)
    pieces = [jnp.zeros((PIECE, LANES), F32)] * STEPS
    for unit in range(UNITS):
        candidate = gathered[unit].astype(F32)
        pieces = [jnp.where(place == unit, candidate, piece) for place, piece in zip(places, pieces)]
    for k in range(STEPS):
        picked[k] = pieces[k].astype(BF16)


def pick_far_kernel(steps, gathered, spread):
    pieces = []
    for k in range(STEPS):
        first = (steps[k] // 8) % 2 == 0
        pieces.append(jnp.where(first, gathered[0, k].astype(F32), gathered[1, k].astype(F32)))
    count = STEPS * PIECE
    row = lax.broadcasted_iota(jnp.int32, (count, count), 0)
    column = lax.broadcasted_iota(jnp.int32, (count, count), 1)
    order = jnp.where(column == (row % SLOTS) * NSEG + row // SLOTS, 1.0, 0.0).astype(BF16)
    ordered = mm(order, jnp.concatenate(pieces, axis=0).astype(BF16)).astype(BF16)
    for part in range(STEPS):
        piece = ordered[part * PIECE : (part + 1) * PIECE]
        for to in range(SPREAD):
            spread[to, part] = piece


def pick(kernel, plan, gathered, shape, name):
    vmem = pl.BlockSpec(memory_space=pltpu.VMEM)
    return pl.pallas_call(
        kernel,
        in_specs=[vmem, vmem],
        out_specs=vmem,
        out_shape=jax.ShapeDtypeStruct(shape, BF16),
        compiler_params=pltpu.CompilerParams(vmem_limit_bytes=VMEM_LIMIT),
        name=name,
    )(plan, gathered)


def correlate_kernel(white, source, table, lagged, own, cross):
    for tile in range(TILES):
        for q in range(2):
            units = white[pl.ds(unit_of(tile, q * LINES), LINES)].astype(F32)
            own[tile, pl.ds(q * (LINES * PIECE), LINES * PIECE), :] = units.reshape(LINES * PIECE, LANES)
    for half in range(2):
        own[TILES + half] = own[half] + own[half + 2]

    for line in range(LINES):
        place = (line // 2) * 8 + line % 2
        for core in range(2):
            for half in range(2):
                right = []
                for part in range(STEPS):
                    both = [source[core, place + tile * 2, part].astype(F32) for tile in (half, half + 2)]
                    for s in range(2):
                        re, im = [x[s * SLOTS : (s + 1) * SLOTS] for x in both]
                        right.append([re, im, re - im])
                for a in range(SB):
                    sums = None
                    for s in range(NSEG):
                        row = pl.ds(a * NSEG + s, 1)
                        left = [own[tile, row, :] for tile in (half, half + 2, half + 4)]
                        terms = [jnp.broadcast_to(x, (SLOTS, LANES)) * y for x, y in zip(left, right[s])]
                        sums = terms if sums is None else [x + y for x, y in zip(sums, terms)]
                    re_re, im_im, mixed = sums
                    rows = pl.ds(core * ROWS + a * SLOTS, SLOTS)
                    cross[line, rows, pl.ds(half * LANES, LANES)] = re_re + im_im
                    cross[line, rows, pl.ds(FREQ + half * LANES, LANES)] = mixed + (im_im - re_re)
        high, low = split(cross[line])
        both = mm_rows(table[...], high)
        out = both[:KEPT] + (both[KEPT:] + mm_rows(table[pl.ds(0, KEPT), :], low))
        for core in range(2):
            part = out[:, core * ROWS : (core + 1) * ROWS]
            lagged[line, core] = pack(part, part[LAST:])


def correlate(*arrays):
    vmem = pl.BlockSpec(memory_space=pltpu.VMEM)
    arrays = arrays + (jnp.asarray(lag_tables()),)
    return pl.pallas_call(
        correlate_kernel,
        in_specs=[vmem] * len(arrays),
        out_specs=vmem,
        out_shape=pltpu.VMEM((LINES, 2, KEPT, ROWS), BF16),
        scratch_shapes=[
            pltpu.VMEM((TILES + 2, ROWS, LANES), F32),
            pltpu.VMEM((LINES, 2 * ROWS, WIDE), F32),
        ],
        compiler_params=pltpu.CompilerParams(vmem_limit_bytes=VMEM_LIMIT),
        name="correlate",
    )(*arrays)


def fold_kernel(parts, keep, send):
    mine = lax.axis_index("w")
    other = 1 - mine
    keep_sum, send_sum = parts[0, mine].astype(F32), parts[0, other].astype(F32)
    for quad in range(1, LINES):
        keep_sum = keep_sum + parts[quad, mine].astype(F32)
        send_sum = send_sum + parts[quad, other].astype(F32)
    keep[...] = unpack(keep_sum)
    send_sum = unpack(send_sum)
    send[...] = pack(send_sum, send_sum[NEAR : NEAR + SLOTS])


def fold(parts):
    vmem = pl.BlockSpec(memory_space=pltpu.VMEM)
    return pl.pallas_call(
        fold_kernel,
        in_specs=[vmem],
        out_specs=[vmem, vmem],
        out_shape=[jax.ShapeDtypeStruct((KEPT, ROWS), F32), jax.ShapeDtypeStruct((KEPT, ROWS), BF16)],
        compiler_params=pltpu.CompilerParams(vmem_limit_bytes=VMEM_LIMIT),
        name="fold",
    )(parts)


def finish_kernel(keep, both, out):
    total = (keep[...] + unpack(both[1 - lax.axis_index("w")].astype(F32))).astype(BF16)
    row = lax.broadcasted_iota(jnp.int32, (ROWS, ROWS), 0)
    column = lax.broadcasted_iota(jnp.int32, (ROWS, ROWS), 1)
    station, slot = (row // 2) % SB, (row // (2 * SB)) * 2 + row % 2
    order = jnp.where(column == station * SLOTS + slot, 1.0, 0.0).astype(BF16)
    out[...] = mm_rows(order, total)[:, :LAGS].astype(BF16).reshape(STEPS, SB, 2, LAGS)


def finish(keep, both):
    vmem = pl.BlockSpec(memory_space=pltpu.VMEM)
    return pl.pallas_call(
        finish_kernel,
        in_specs=[vmem, vmem],
        out_specs=vmem,
        out_shape=jax.ShapeDtypeStruct((STEPS, SB, 2, LAGS), BF16),
        compiler_params=pltpu.CompilerParams(vmem_limit_bytes=VMEM_LIMIT),
        name="finish",
    )(keep, both)


def shards(records, masks, plan):
    white, steps = whiten(records.reshape(ROWS, SEGLEN), masks[0].T, plan)
    pieces = lax.all_to_all(white, ("q", "x", "r", "c"), 0, 0, tiled=True)
    picked = pick(pick_near_kernel, steps, pieces, (STEPS, PIECE, LANES), "pick_near")
    ends = lax.all_gather(picked, "p", axis=0, tiled=False)
    spread = pick(pick_far_kernel, steps, ends, (SPREAD, STEPS, PIECE, LANES), "pick_far")
    near = lax.all_to_all(spread, ("q", "x", "r"), 0, 0, tiled=True)
    source = lax.all_gather(near, "c", axis=0, tiled=False)
    lagged = correlate(white, source)
    parts = lax.all_to_all(lagged, "y", 0, 0, tiled=True)
    keep, send = fold(parts)
    both = lax.all_gather(send, "w", axis=0, tiled=False)
    return finish(keep, both)


def solution(mesh):
    grid = Mesh(mesh.devices.reshape(4, 2, 4, 2, 2, 2, 2), ("y", "w", "x", "p", "q", "r", "c"))
    hour = ("y", "w")
    sta = ("x", "p", "q", "r", "c")
    return jax.shard_map(
        shards,
        mesh=grid,
        in_specs=(P(hour, sta, None, None), P(hour, sta, None), P()),
        out_specs=P(None, sta, hour, None),
        check_vma=False,
    )
```

```python
import math

import jax
import jax.numpy as jnp
import numpy as np
from jax import lax
from jax.experimental import pallas as pl
from jax.experimental.pallas import tpu as pltpu
from jax.sharding import Mesh, PartitionSpec as P

SB = 16
NSEG = 8
SEGLEN = 512
FREQ = 256
LAGS = 201
STEPS = 4
HOURS = 8
ROWS = SB * NSEG
WIDE = 2 * FREQ
LANES = 128
PIECE = 2 * NSEG
TILES = WIDE // LANES
UNITS = 32
LINES = 4
SPREAD = 16
PARTS = 4
SLOTS = 2 * STEPS
KEPT = 208
LAST = KEPT - SLOTS
NEAR = LAGS // 2 - SLOTS // 2

F32 = jnp.float32
BF16 = jnp.bfloat16
VMEM_LIMIT = 16 * 1024 * 1024


def angle_rows(times):
    product = (times * lax.broadcasted_iota(jnp.int32, times.shape, 1)) % SEGLEN
    angles = product.astype(F32) * (2.0 * math.pi / SEGLEN)
    return jnp.cos(angles), -jnp.sin(angles)


def lag_tables():
    shifts = np.arange(LAGS) - LAGS // 2
    angles = 2.0 * math.pi * ((shifts[:, None] * np.arange(FREQ)[None, :]) % SEGLEN) / SEGLEN
    table = np.concatenate([np.cos(angles), -np.sin(angles)], axis=1) / math.sqrt(NSEG * FREQ * HOURS)
    table = np.concatenate([table, table[NEAR + 1 : NEAR + SLOTS]], axis=0)
    high = table.astype(BF16)
    return np.concatenate([high, (table - high.astype(np.float64)).astype(BF16)], axis=0)


def mm(left, right):
    return jnp.dot(left, right, preferred_element_type=F32)


def mm_rows(left, right):
    return lax.dot_general(left, right, (((1,), (1,)), ((), ())), preferred_element_type=F32)


def spare():
    return lax.broadcasted_iota(jnp.int32, (SLOTS, ROWS), 0) > 0


def pack(value, near):
    high = value.astype(BF16)
    rest = near - near.astype(BF16).astype(F32)
    last = jnp.where(spare(), rest, value[LAST:])
    return jnp.concatenate([high[: LAST - SLOTS], jnp.concatenate([value[LAST - SLOTS : LAST], last], axis=0).astype(BF16)], axis=0)


def unpack(value):
    near = value[NEAR : NEAR + SLOTS] + jnp.where(spare(), value[LAST:], 0.0)
    return jnp.concatenate([value[:NEAR], near, value[NEAR + SLOTS :]], axis=0)


def split(value):
    high = value.astype(BF16)
    return high, (value - high.astype(F32)).astype(BF16)


def band(length, reach):
    first = lax.broadcasted_iota(jnp.int32, (length, length), 0)
    second = lax.broadcasted_iota(jnp.int32, (length, length), 1)
    matrix = jnp.where(jnp.abs(first - second) <= reach, 1.0, 0.0).astype(BF16)
    place = lax.broadcasted_iota(jnp.int32, (1, length), 1)
    count = jnp.minimum(place + reach, length - 1) - jnp.maximum(place - reach, 0) + 1
    return matrix, count.astype(F32)


def unit_of(tile, pair):
    return (pair // LINES) * (TILES * LINES) + tile * LINES + pair % LINES


def whiten_kernel(records, mask, plan, white, steps, raw_buffer, mask_buffer, plan_buffer, trig, sems):
    fetches = []
    for part in range(PARTS):
        rows = pl.ds(part * (ROWS // PARTS), ROWS // PARTS)
        fetches.append(pltpu.make_async_copy(records.at[rows], raw_buffer.at[rows], sems.at[part]))
    fetches.append(pltpu.make_async_copy(mask, mask_buffer, sems.at[PARTS]))
    fetches.append(pltpu.make_async_copy(plan, plan_buffer, sems.at[PARTS + 1]))
    for fetch in fetches:
        fetch.start()
    row = lax.broadcasted_iota(jnp.int32, (NSEG, FREQ), 0)
    cos, sin = angle_rows(row)
    turns_cos, turns_sin = angle_rows(lax.shift_left(jnp.full_like(row, NSEG), row))
    trig[pl.ds(0, NSEG), :FREQ] = cos
    trig[pl.ds(0, NSEG), FREQ:] = sin
    size, level = NSEG, 0
    while size < SEGLEN:
        cos, sin = trig[pl.ds(0, size), :FREQ], trig[pl.ds(0, size), FREQ:]
        turn_cos, turn_sin = turns_cos[level : level + 1], turns_sin[level : level + 1]
        trig[pl.ds(size, size), :FREQ] = cos * turn_cos - sin * turn_sin
        trig[pl.ds(size, size), FREQ:] = sin * turn_cos + cos * turn_sin
        size, level = 2 * size, level + 1
    table_high, table_low = split(trig[...])
    time_band, time_count = band(SEGLEN, SEGLEN // 8)
    freq_band, freq_count = band(FREQ, FREQ // 4)
    for fetch in fetches:
        fetch.wait()
    raw = raw_buffer[...]
    envelope = mm(jnp.abs(raw), time_band) / time_count + 1e-06
    high, low = split(raw.astype(F32) / envelope)
    spec = mm(high, table_high) + (mm(low, table_high) + mm(high, table_low))
    spec_re, spec_im = spec[:, :FREQ], spec[:, FREQ:]
    magnitude = jnp.sqrt(spec_re * spec_re + spec_im * spec_im)
    high, low = split(magnitude)
    smooth = (mm(high, freq_band) + mm(low, freq_band)) / freq_count + 1e-06
    station = lax.broadcasted_iota(jnp.int32, (SB, NSEG, SB), 0)
    column = lax.broadcasted_iota(jnp.int32, (SB, NSEG, SB), 2)
    spread = jnp.where(station == column, mask_buffer[...].astype(F32)[None], 0.0)
    valid = jnp.sum(spread, axis=2, keepdims=True)
    weight = (valid / smooth.reshape(SB, NSEG, FREQ)).reshape(ROWS, FREQ)
    for tile in range(TILES):
        spec_part = (spec_re, spec_im)[tile // 2]
        lanes = slice((tile % 2) * LANES, (tile % 2 + 1) * LANES)
        part = (spec_part[:, lanes] * weight[:, lanes]).astype(BF16)
        for group in range(ROWS // PIECE):
            white[unit_of(tile, group)] = part[group * PIECE : (group + 1) * PIECE]
    for k in range(STEPS):
        steps[k] = jnp.full((PIECE, LANES), plan_buffer[k], jnp.int32)


def whiten(records, masks, plan):
    hbm = pl.BlockSpec(memory_space=pltpu.HBM)
    vmem = pl.BlockSpec(memory_space=pltpu.VMEM)
    return pl.pallas_call(
        whiten_kernel,
        in_specs=[hbm] * 3,
        out_specs=[vmem] * 2,
        out_shape=[pltpu.VMEM((UNITS, PIECE, LANES), BF16), pltpu.VMEM((STEPS, PIECE, LANES), jnp.int32)],
        scratch_shapes=[
            pltpu.VMEM((ROWS, SEGLEN), BF16),
            pltpu.VMEM((NSEG, SB), jnp.int32),
            pltpu.SMEM((STEPS,), jnp.int32),
            pltpu.VMEM((SEGLEN, WIDE), F32),
            pltpu.SemaphoreType.DMA((PARTS + 2,)),
        ],
        compiler_params=pltpu.CompilerParams(vmem_limit_bytes=VMEM_LIMIT),
        name="whiten",
    )(*(pltpu.with_memory_space_constraint(x, pltpu.HBM) for x in (records, masks, plan)))


def pick_near_kernel(steps, gathered, picked):
    places = []
    for k in range(STEPS):
        block = steps[k]
        q, x, rc = (block // 4) % 2, block // 16, block % 4
        places.append(q * 16 + x * 4 + rc)
    pieces = [jnp.zeros((PIECE, LANES), F32)] * STEPS
    for unit in range(UNITS):
        candidate = gathered[unit].astype(F32)
        pieces = [jnp.where(place == unit, candidate, piece) for place, piece in zip(places, pieces)]
    for k in range(STEPS):
        picked[k] = pieces[k].astype(BF16)


def pick_far_kernel(steps, gathered, spread):
    pieces = []
    for k in range(STEPS):
        first = (steps[k] // 8) % 2 == 0
        pieces.append(jnp.where(first, gathered[0, k].astype(F32), gathered[1, k].astype(F32)))
    count = STEPS * PIECE
    row = lax.broadcasted_iota(jnp.int32, (count, count), 0)
    column = lax.broadcasted_iota(jnp.int32, (count, count), 1)
    order = jnp.where(column == (row % SLOTS) * NSEG + row // SLOTS, 1.0, 0.0).astype(BF16)
    ordered = mm(order, jnp.concatenate(pieces, axis=0).astype(BF16)).astype(BF16)
    for part in range(STEPS):
        piece = ordered[part * PIECE : (part + 1) * PIECE]
        for to in range(SPREAD):
            spread[to, part] = piece


def pick(kernel, plan, gathered, shape, name):
    vmem = pl.BlockSpec(memory_space=pltpu.VMEM)
    return pl.pallas_call(
        kernel,
        in_specs=[vmem, vmem],
        out_specs=vmem,
        out_shape=jax.ShapeDtypeStruct(shape, BF16),
        compiler_params=pltpu.CompilerParams(vmem_limit_bytes=VMEM_LIMIT),
        name=name,
    )(plan, gathered)


def correlate_kernel(white, source, table, lagged, own, cross):
    for tile in range(TILES):
        for q in range(2):
            units = white[pl.ds(unit_of(tile, q * LINES), LINES)].astype(F32)
            own[tile, pl.ds(q * (LINES * PIECE), LINES * PIECE), :] = units.reshape(LINES * PIECE, LANES)
    for half in range(2):
        own[TILES + half] = own[half] + own[half + 2]

    for line in range(LINES):
        place = (line // 2) * 8 + line % 2
        for core in range(2):
            for half in range(2):
                right = []
                for part in range(STEPS):
                    both = [source[core, place + tile * 2, part].astype(F32) for tile in (half, half + 2)]
                    for s in range(2):
                        re, im = [x[s * SLOTS : (s + 1) * SLOTS] for x in both]
                        right.append([re, im, re - im])
                for a in range(SB):
                    sums = None
                    for s in range(NSEG):
                        row = pl.ds(a * NSEG + s, 1)
                        left = [own[tile, row, :] for tile in (half, half + 2, half + 4)]
                        terms = [jnp.broadcast_to(x, (SLOTS, LANES)) * y for x, y in zip(left, right[s])]
                        sums = terms if sums is None else [x + y for x, y in zip(sums, terms)]
                    re_re, im_im, mixed = sums
                    rows = pl.ds(core * ROWS + a * SLOTS, SLOTS)
                    cross[line, rows, pl.ds(half * LANES, LANES)] = re_re + im_im
                    cross[line, rows, pl.ds(FREQ + half * LANES, LANES)] = mixed + (im_im - re_re)
        high, low = split(cross[line])
        both = mm_rows(table[...], high)
        out = both[:KEPT] + (both[KEPT:] + mm_rows(table[pl.ds(0, KEPT), :], low))
        for core in range(2):
            part = out[:, core * ROWS : (core + 1) * ROWS]
            lagged[line, core] = pack(part, part[LAST:])


def correlate(*arrays):
    vmem = pl.BlockSpec(memory_space=pltpu.VMEM)
    arrays = arrays + (jnp.asarray(lag_tables()),)
    return pl.pallas_call(
        correlate_kernel,
        in_specs=[vmem] * len(arrays),
        out_specs=vmem,
        out_shape=pltpu.VMEM((LINES, 2, KEPT, ROWS), BF16),
        scratch_shapes=[
            pltpu.VMEM((TILES + 2, ROWS, LANES), F32),
            pltpu.VMEM((LINES, 2 * ROWS, WIDE), F32),
        ],
        compiler_params=pltpu.CompilerParams(vmem_limit_bytes=VMEM_LIMIT),
        name="correlate",
    )(*arrays)


def fold_kernel(parts, keep, send):
    mine = lax.axis_index("w")
    other = 1 - mine
    keep_sum, send_sum = parts[0, mine].astype(F32), parts[0, other].astype(F32)
    for quad in range(1, LINES):
        keep_sum = keep_sum + parts[quad, mine].astype(F32)
        send_sum = send_sum + parts[quad, other].astype(F32)
    keep[...] = unpack(keep_sum)
    send_sum = unpack(send_sum)
    send[...] = pack(send_sum, send_sum[NEAR : NEAR + SLOTS])


def fold(parts):
    vmem = pl.BlockSpec(memory_space=pltpu.VMEM)
    return pl.pallas_call(
        fold_kernel,
        in_specs=[vmem],
        out_specs=[vmem, vmem],
        out_shape=[jax.ShapeDtypeStruct((KEPT, ROWS), F32), jax.ShapeDtypeStruct((KEPT, ROWS), BF16)],
        compiler_params=pltpu.CompilerParams(vmem_limit_bytes=VMEM_LIMIT),
        name="fold",
    )(parts)


def finish_kernel(keep, both, out):
    total = (keep[...] + unpack(both[1 - lax.axis_index("w")].astype(F32))).astype(BF16)
    row = lax.broadcasted_iota(jnp.int32, (ROWS, ROWS), 0)
    column = lax.broadcasted_iota(jnp.int32, (ROWS, ROWS), 1)
    station, slot = (row // 2) % SB, (row // (2 * SB)) * 2 + row % 2
    order = jnp.where(column == station * SLOTS + slot, 1.0, 0.0).astype(BF16)
    out[...] = mm_rows(order, total)[:, :LAGS].astype(BF16).reshape(STEPS, SB, 2, LAGS)


def finish(keep, both):
    vmem = pl.BlockSpec(memory_space=pltpu.VMEM)
    return pl.pallas_call(
        finish_kernel,
        in_specs=[vmem, vmem],
        out_specs=vmem,
        out_shape=jax.ShapeDtypeStruct((STEPS, SB, 2, LAGS), BF16),
        compiler_params=pltpu.CompilerParams(vmem_limit_bytes=VMEM_LIMIT),
        name="finish",
    )(keep, both)


def shards(records, masks, plan):
    white, steps = whiten(records.reshape(ROWS, SEGLEN), masks[0].T, plan)
    pieces = lax.all_to_all(white, ("q", "x", "r", "c"), 0, 0, tiled=True)
    picked = pick(pick_near_kernel, steps, pieces, (STEPS, PIECE, LANES), "pick_near")
    ends = lax.all_gather(picked, "p", axis=0, tiled=False)
    spread = pick(pick_far_kernel, steps, ends, (SPREAD, STEPS, PIECE, LANES), "pick_far")
    near = lax.all_to_all(spread, ("q", "x", "r"), 0, 0, tiled=True)
    source = lax.all_gather(near, "c", axis=0, tiled=False)
    lagged = correlate(white, source)
    parts = lax.all_to_all(lagged, "y", 0, 0, tiled=True)
    keep, send = fold(parts)
    both = lax.all_gather(send, "w", axis=0, tiled=False)
    return finish(keep, both)


def solution(mesh):
    grid = Mesh(mesh.devices.reshape(4, 2, 4, 2, 2, 2, 2), ("y", "w", "x", "p", "q", "r", "c"))
    hour = ("y", "w")
    sta = ("x", "p", "q", "r", "c")
    return jax.shard_map(
        shards,
        mesh=grid,
        in_specs=(P(hour, sta, None, None), P(hour, sta, None), P()),
        out_specs=P(None, sta, hour, None),
        check_vma=False,
    )
```

```python
import math

import jax
import jax.numpy as jnp
import numpy as np
from jax import lax
from jax.experimental import pallas as pl
from jax.experimental.pallas import tpu as pltpu
from jax.sharding import Mesh, PartitionSpec as P

SB = 16
NSEG = 8
SEGLEN = 512
FREQ = 256
LAGS = 201
STEPS = 4
HOURS = 8
ROWS = SB * NSEG
WIDE = 2 * FREQ
LANES = 128
PIECE = 2 * NSEG
TILES = WIDE // LANES
UNITS = 32
LINES = 4
SPREAD = 16
SLOTS = 2 * STEPS
KEPT = 208
LAST = KEPT - SLOTS
NEAR = LAGS // 2 - SLOTS // 2

F32 = jnp.float32
BF16 = jnp.bfloat16
VMEM_LIMIT = 16 * 1024 * 1024


def angle_rows(times):
    product = (times * lax.broadcasted_iota(jnp.int32, times.shape, 1)) % SEGLEN
    angles = product.astype(F32) * (2.0 * math.pi / SEGLEN)
    return jnp.cos(angles), -jnp.sin(angles)


def lag_tables():
    shifts = np.arange(LAGS) - LAGS // 2
    angles = 2.0 * math.pi * ((shifts[:, None] * np.arange(FREQ)[None, :]) % SEGLEN) / SEGLEN
    table = np.concatenate([np.cos(angles), -np.sin(angles)], axis=1) / math.sqrt(NSEG * FREQ * HOURS)
    table = np.concatenate([table, table[NEAR + 1 : NEAR + SLOTS]], axis=0)
    high = table.astype(BF16)
    return np.concatenate([high, (table - high.astype(np.float64)).astype(BF16)], axis=0)


def mm(left, right):
    return jnp.dot(left, right, preferred_element_type=F32)


def mm_rows(left, right):
    return lax.dot_general(left, right, (((1,), (1,)), ((), ())), preferred_element_type=F32)


def spare():
    return lax.broadcasted_iota(jnp.int32, (SLOTS, ROWS), 0) > 0


def pack(value, near):
    high = value.astype(BF16)
    rest = near - near.astype(BF16).astype(F32)
    last = jnp.where(spare(), rest, value[LAST:])
    return jnp.concatenate([high[: LAST - SLOTS], jnp.concatenate([value[LAST - SLOTS : LAST], last], axis=0).astype(BF16)], axis=0)


def unpack(value):
    near = value[NEAR : NEAR + SLOTS] + jnp.where(spare(), value[LAST:], 0.0)
    return jnp.concatenate([value[:NEAR], near, value[NEAR + SLOTS :]], axis=0)


def split(value):
    high = value.astype(BF16)
    return high, (value - high.astype(F32)).astype(BF16)


def band(length, reach):
    first = lax.broadcasted_iota(jnp.int32, (length, length), 0)
    second = lax.broadcasted_iota(jnp.int32, (length, length), 1)
    matrix = jnp.where(jnp.abs(first - second) <= reach, 1.0, 0.0).astype(BF16)
    place = lax.broadcasted_iota(jnp.int32, (1, length), 1)
    count = jnp.minimum(place + reach, length - 1) - jnp.maximum(place - reach, 0) + 1
    return matrix, count.astype(F32)


def crossed(pair):
    end = lax.axis_index("p")
    return pair + (end if pair % 2 == 0 else -end)


def slot_of(tile, pair):
    return (pair // LINES) * (TILES * LINES) + tile * LINES + crossed(pair % LINES)


def whiten_kernel(records, mask, plan, white, steps, raw_buffer, mask_buffer, plan_buffer, trig, sems):
    fetches = [
        pltpu.make_async_copy(records, raw_buffer, sems.at[0]),
        pltpu.make_async_copy(mask, mask_buffer, sems.at[1]),
        pltpu.make_async_copy(plan, plan_buffer, sems.at[2]),
    ]
    for fetch in fetches:
        fetch.start()
    row = lax.broadcasted_iota(jnp.int32, (NSEG, FREQ), 0)
    cos, sin = angle_rows(row)
    turns_cos, turns_sin = angle_rows(lax.shift_left(jnp.full_like(row, NSEG), row))
    trig[pl.ds(0, NSEG), :FREQ] = cos
    trig[pl.ds(0, NSEG), FREQ:] = sin
    size, level = NSEG, 0
    while size < SEGLEN:
        cos, sin = trig[pl.ds(0, size), :FREQ], trig[pl.ds(0, size), FREQ:]
        turn_cos, turn_sin = turns_cos[level : level + 1], turns_sin[level : level + 1]
        trig[pl.ds(size, size), :FREQ] = cos * turn_cos - sin * turn_sin
        trig[pl.ds(size, size), FREQ:] = sin * turn_cos + cos * turn_sin
        size, level = 2 * size, level + 1
    table_high, table_low = split(trig[...])
    time_band, time_count = band(SEGLEN, SEGLEN // 8)
    freq_band, freq_count = band(FREQ, FREQ // 4)
    for fetch in fetches:
        fetch.wait()
    raw = raw_buffer[...]
    envelope = mm(jnp.abs(raw), time_band) / time_count + 1e-06
    high, low = split(raw.astype(F32) / envelope)
    spec = mm(high, table_high) + (mm(low, table_high) + mm(high, table_low))
    spec_re, spec_im = spec[:, :FREQ], spec[:, FREQ:]
    magnitude = jnp.sqrt(spec_re * spec_re + spec_im * spec_im)
    high, low = split(magnitude)
    smooth = (mm(high, freq_band) + mm(low, freq_band)) / freq_count + 1e-06
    station = lax.broadcasted_iota(jnp.int32, (SB, NSEG, SB), 0)
    column = lax.broadcasted_iota(jnp.int32, (SB, NSEG, SB), 2)
    spread = jnp.where(station == column, mask_buffer[...].astype(F32)[None], 0.0)
    valid = jnp.sum(spread, axis=2, keepdims=True)
    weight = (valid / smooth.reshape(SB, NSEG, FREQ)).reshape(ROWS, FREQ)
    for tile in range(TILES):
        spec_part = (spec_re, spec_im)[tile // 2]
        lanes = slice((tile % 2) * LANES, (tile % 2 + 1) * LANES)
        part = (spec_part[:, lanes] * weight[:, lanes]).astype(BF16)
        for group in range(ROWS // PIECE):
            white[slot_of(tile, group)] = part[group * PIECE : (group + 1) * PIECE]
    for k in range(STEPS):
        steps[k] = jnp.full((PIECE, LANES), plan_buffer[k], jnp.int32)


def whiten(records, masks, plan):
    hbm = pl.BlockSpec(memory_space=pltpu.HBM)
    vmem = pl.BlockSpec(memory_space=pltpu.VMEM)
    return pl.pallas_call(
        whiten_kernel,
        in_specs=[hbm] * 3,
        out_specs=[vmem] * 2,
        out_shape=[pltpu.VMEM((UNITS, PIECE, LANES), BF16), pltpu.VMEM((STEPS, PIECE, LANES), jnp.int32)],
        scratch_shapes=[
            pltpu.VMEM((ROWS, SEGLEN), BF16),
            pltpu.VMEM((NSEG, SB), jnp.int32),
            pltpu.SMEM((STEPS,), jnp.int32),
            pltpu.VMEM((SEGLEN, WIDE), F32),
            pltpu.SemaphoreType.DMA((3,)),
        ],
        compiler_params=pltpu.CompilerParams(vmem_limit_bytes=VMEM_LIMIT),
        name="whiten",
    )(*(pltpu.with_memory_space_constraint(x, pltpu.HBM) for x in (records, masks, plan)))


def pick_near_kernel(steps, gathered, picked):
    places = []
    for k in range(STEPS):
        block = steps[k]
        q, x, rc = (block // 4) % 2, block // 16, block % 4
        places.append(q * 16 + x * 4 + rc)
    pieces = [jnp.zeros((PIECE, LANES), F32)] * STEPS
    for unit in range(UNITS):
        candidate = gathered[unit].astype(F32)
        pieces = [jnp.where(place == unit, candidate, piece) for place, piece in zip(places, pieces)]
    for k in range(STEPS):
        picked[k] = pieces[k].astype(BF16)


def pick_far_kernel(steps, gathered, spread):
    pieces = []
    for k in range(STEPS):
        first = (steps[k] // 8) % 2 == 0
        pieces.append(jnp.where(first, gathered[0, k].astype(F32), gathered[1, k].astype(F32)))
    count = STEPS * PIECE
    row = lax.broadcasted_iota(jnp.int32, (count, count), 0)
    column = lax.broadcasted_iota(jnp.int32, (count, count), 1)
    order = jnp.where(column == (row % SLOTS) * NSEG + row // SLOTS, 1.0, 0.0).astype(BF16)
    ordered = mm(order, jnp.concatenate(pieces, axis=0).astype(BF16)).astype(BF16)
    for part in range(STEPS):
        piece = ordered[part * PIECE : (part + 1) * PIECE]
        for to in range(SPREAD):
            spread[to, part] = piece


def pick(kernel, plan, gathered, shape, name):
    vmem = pl.BlockSpec(memory_space=pltpu.VMEM)
    return pl.pallas_call(
        kernel,
        in_specs=[vmem, vmem],
        out_specs=vmem,
        out_shape=jax.ShapeDtypeStruct(shape, BF16),
        compiler_params=pltpu.CompilerParams(vmem_limit_bytes=VMEM_LIMIT),
        name=name,
    )(plan, gathered)


def correlate_kernel(white, source, table, lagged, own, cross):
    for tile in range(TILES):
        for pair in range(ROWS // PIECE):
            own[tile, pl.ds(pair * PIECE, PIECE), :] = white[slot_of(tile, pair)].astype(F32)
    for half in range(2):
        own[TILES + half] = own[half] + own[half + 2]

    for line in range(LINES):
        place = (line // 2) * 8 + line % 2
        for core in range(2):
            for half in range(2):
                right = []
                for part in range(STEPS):
                    both = [source[core, place + tile * 2, part].astype(F32) for tile in (half, half + 2)]
                    for s in range(2):
                        re, im = [x[s * SLOTS : (s + 1) * SLOTS] for x in both]
                        right.append([re, im, re - im])
                for a in range(SB):
                    sums = None
                    for s in range(NSEG):
                        row = pl.ds(a * NSEG + s, 1)
                        left = [own[tile, row, :] for tile in (half, half + 2, half + 4)]
                        terms = [jnp.broadcast_to(x, (SLOTS, LANES)) * y for x, y in zip(left, right[s])]
                        sums = terms if sums is None else [x + y for x, y in zip(sums, terms)]
                    re_re, im_im, mixed = sums
                    rows = pl.ds(core * ROWS + a * SLOTS, SLOTS)
                    cross[line, rows, pl.ds(half * LANES, LANES)] = re_re + im_im
                    cross[line, rows, pl.ds(FREQ + half * LANES, LANES)] = mixed + (im_im - re_re)
        high, low = split(cross[line])
        both = mm_rows(table[...], high)
        out = both[:KEPT] + (both[KEPT:] + mm_rows(table[pl.ds(0, KEPT), :], low))
        for core in range(2):
            part = out[:, core * ROWS : (core + 1) * ROWS]
            lagged[line, crossed(core)] = pack(part, part[LAST:])


def correlate(*arrays):
    vmem = pl.BlockSpec(memory_space=pltpu.VMEM)
    arrays = arrays + (jnp.asarray(lag_tables()),)
    return pl.pallas_call(
        correlate_kernel,
        in_specs=[vmem] * len(arrays),
        out_specs=vmem,
        out_shape=pltpu.VMEM((LINES, 2, KEPT, ROWS), BF16),
        scratch_shapes=[
            pltpu.VMEM((TILES + 2, ROWS, LANES), F32),
            pltpu.VMEM((LINES, 2 * ROWS, WIDE), F32),
        ],
        compiler_params=pltpu.CompilerParams(vmem_limit_bytes=VMEM_LIMIT),
        name="correlate",
    )(*arrays)


def fold_kernel(parts, keep, send):
    mine = lax.axis_index("w")
    other = 1 - mine
    keep_sum, send_sum = parts[0, mine].astype(F32), parts[0, other].astype(F32)
    for quad in range(1, LINES):
        keep_sum = keep_sum + parts[quad, mine].astype(F32)
        send_sum = send_sum + parts[quad, other].astype(F32)
    keep[...] = unpack(keep_sum)
    send_sum = unpack(send_sum)
    send[...] = pack(send_sum, send_sum[NEAR : NEAR + SLOTS])


def fold(parts):
    vmem = pl.BlockSpec(memory_space=pltpu.VMEM)
    return pl.pallas_call(
        fold_kernel,
        in_specs=[vmem],
        out_specs=[vmem, vmem],
        out_shape=[jax.ShapeDtypeStruct((KEPT, ROWS), F32), jax.ShapeDtypeStruct((KEPT, ROWS), BF16)],
        compiler_params=pltpu.CompilerParams(vmem_limit_bytes=VMEM_LIMIT),
        name="fold",
    )(parts)


def finish_kernel(keep, both, out):
    total = (keep[...] + unpack(both[1 - lax.axis_index("w")].astype(F32))).astype(BF16)
    row = lax.broadcasted_iota(jnp.int32, (ROWS, ROWS), 0)
    column = lax.broadcasted_iota(jnp.int32, (ROWS, ROWS), 1)
    station, slot = (row // 2) % SB, (row // (2 * SB)) * 2 + row % 2
    order = jnp.where(column == station * SLOTS + slot, 1.0, 0.0).astype(BF16)
    out[...] = mm_rows(order, total)[:, :LAGS].astype(BF16).reshape(STEPS, SB, 2, LAGS)


def finish(keep, both):
    vmem = pl.BlockSpec(memory_space=pltpu.VMEM)
    return pl.pallas_call(
        finish_kernel,
        in_specs=[vmem, vmem],
        out_specs=vmem,
        out_shape=jax.ShapeDtypeStruct((STEPS, SB, 2, LAGS), BF16),
        compiler_params=pltpu.CompilerParams(vmem_limit_bytes=VMEM_LIMIT),
        name="finish",
    )(keep, both)


def shards(records, masks, plan):
    white, steps = whiten(records.reshape(ROWS, SEGLEN), masks[0].T, plan)
    pieces = lax.all_to_all(white, ("q", "x", "r", "c"), 0, 0, tiled=True)
    picked = pick(pick_near_kernel, steps, pieces, (STEPS, PIECE, LANES), "pick_near")
    ends = lax.all_gather(picked, ("p", "c"), axis=0, tiled=False, axis_index_groups=[[0, 3], [1, 2]])
    spread = pick(pick_far_kernel, steps, ends, (SPREAD, STEPS, PIECE, LANES), "pick_far")
    near = lax.all_to_all(spread, ("q", "x", "r"), 0, 0, tiled=True)
    source = lax.all_gather(near, "c", axis=0, tiled=False)
    lagged = correlate(white, source)
    parts = lax.all_to_all(lagged, "y", 0, 0, tiled=True)
    keep, send = fold(parts)
    both = lax.all_gather(send, "w", axis=0, tiled=False)
    return finish(keep, both)


def solution(mesh):
    grid = Mesh(mesh.devices.reshape(4, 2, 4, 2, 2, 2, 2), ("y", "w", "x", "p", "q", "r", "c"))
    hour = ("y", "w")
    sta = ("x", "p", "q", "r", "c")
    return jax.shard_map(
        shards,
        mesh=grid,
        in_specs=(P(hour, sta, None, None), P(hour, sta, None), P()),
        out_specs=P(None, sta, hour, None),
        check_vma=False,
    )
```
